32 devices in a mesh: gx: 8 (over y, x, core), gy: 4 (over z).
Axes of the slice: x: 2, y: 2, z: 4, core: 2. Of those that a mesh axis runs over, the one named last changes fastest.
Arguments:
- density: float32 [16, 64, 128], P('gx', 'gy'), may hold values from 0.8 to 1.6
- momentum: float32 [3, 16, 64, 128], P(None, 'gx', 'gy'), may hold values from -0.4 to 0.4
- energy: float32 [16, 64, 128], P('gx', 'gy'), may hold values from 2 to 3
- forcing: float32 [5, 16, 64, 128], P(None, 'gx', 'gy'), may hold values from -6 to 6
- coupling: float32 [2, 5, 5], replicated, may hold values from 0.22 to 1.1
- inverse: float32 [5, 5], replicated, may hold values from 0.09 to 0.63
Outputs:
- state_new: float32 [5, 16, 64, 128], P(None, 'gx', 'gy')
The draws below stay inside these ranges and needn't reach their ends.
All inputs are finite; a program needn't handle non-finite values.
Results may differ from the reference program's by a relative error of at most 0.0003.
Values sent between devices are 32-bit elements; how exact they have to be, the bound alone decides.
A program may use at most 64 MiB of HBM per device.

```python
import jax
import jax.numpy as jnp
from jax import lax

VARS = 5
NZ = 128
NX = 16
NY = 64


def draw_inverse(key, part):
    key = jax.random.fold_in(key, 7)
    key_diag, key_off = jax.random.split(key)
    diag_part = jax.random.uniform(key_diag, (VARS,), jnp.float32, 0.53, 0.61)
    off_part = jax.random.uniform(key_off, (VARS, VARS), jnp.float32, 0.09, 0.11)
    identity = jnp.eye(VARS, dtype=jnp.float32)
    return identity * diag_part[None, :] + (1.0 - identity) * off_part


def draw_coupling(key, part):
    key = jax.random.fold_in(key, 11)
    key_diag, key_off = jax.random.split(key)
    diag_part = jax.random.uniform(key_diag, (2, VARS), jnp.float32, 1.0, 1.1)
    off_part = jax.random.uniform(key_off, (2, VARS, VARS), jnp.float32, 0.22, 0.28)
    identity = jnp.eye(VARS, dtype=jnp.float32)[None]
    return identity * diag_part[:, None, :] + (1.0 - identity) * off_part


def draw_momentum(key, part):
    key = jax.random.fold_in(key, 13)
    values = jnp.clip(0.15 * jax.random.normal(key, (3, NX, NY, NZ), jnp.float32), -0.4, 0.4)
    return values


def shard_levels(rng, dims, cuts, smallest, largest):
    loudness, own = 1.0, jax.random.fold_in(rng, 6)
    for position, shards_of in cuts:
        heights = jnp.exp(jax.random.uniform(jax.random.fold_in(own, position), (shards_of,), jnp.float32, smallest / len(cuts), largest / len(cuts)))
        loudness = loudness * jnp.repeat(heights, dims[position] // shards_of).reshape([-1 if axis == position else 1 for axis in range(len(dims))])
    return loudness


def centred(key, shape, width, reach, pieces=(), held_as=jnp.bfloat16):
    drawn = width * jax.random.normal(key, shape, jnp.float32)
    if pieces:
        drawn = drawn * shard_levels(key, shape, pieces, -0.22, 0.18)
    return jnp.clip(drawn, -reach, reach).astype(held_as)


def setup_inputs(seed: int = 0) -> dict:
    keys = jax.random.split(jax.random.key(seed), 7)
    density = jnp.clip(0.8 + 0.8 * jax.random.uniform(keys[0], (NX, NY, NZ), jnp.float32) ** shard_levels(keys[0], (NX, NY, NZ), ((0, 8), (1, 4)), -0.2, 0.2), 0.8, 1.6)
    momentum = draw_momentum(jax.random.fold_in(keys[6], 71), 0)
    energy = jnp.clip(2.0 + 1.0 * jax.random.uniform(keys[2], (NX, NY, NZ), jnp.float32) ** shard_levels(keys[2], (NX, NY, NZ), ((0, 8), (1, 4)), -0.2, 0.2), 2.0, 3.0)
    forcing = centred(keys[3], (VARS, NX, NY, NZ), 1.0, 6.0, ((1, 8), (2, 4)), jnp.float32)
    coupling = draw_coupling(jax.random.fold_in(keys[6], 71), 0)
    inverse = draw_inverse(jax.random.fold_in(keys[6], 71), 0)
    return dict(density=density, momentum=momentum, energy=energy, forcing=forcing, coupling=coupling, inverse=inverse)


precision_high = lax.Precision.HIGHEST
beta_coupling = 0.25
dissipation = 0.05


def apply_block(matrix, field):
    return jnp.einsum('ab,b...->a...', matrix, field, precision=precision_high)


def flux_direction(state, direction):
    density_safe = jnp.where(state[0] > 0.1, state[0], 1.0)
    momentum = state[1:4]
    energy = state[4]
    pressure = 0.4 * (energy - 0.5 * jnp.sum(momentum * momentum, axis=0) / density_safe)
    velocity = momentum[direction] / density_safe
    components = [momentum[direction]]
    for component in range(3):
        extra = pressure if component == direction else 0.0
        components.append(momentum[component] * velocity + extra)
    components.append((energy + pressure) * velocity)
    return jnp.stack(components)


def offset_core(array, axis, offset):
    lead_dims = array.ndim - 3
    slicer = [slice(None)] * lead_dims + [slice(2, -2), slice(2, -2), slice(2, -2)]
    length = array.shape[lead_dims + axis]
    slicer[lead_dims + axis] = slice(2 + offset, length - 2 + offset)
    return array[tuple(slicer)]


def residual_rhs(ext_state, forcing):
    residual_sum = forcing
    for direction in range(3):
        flux_dir = flux_direction(ext_state, direction)
        residual_sum = residual_sum - 0.5 * (offset_core(flux_dir, direction, 1) - offset_core(flux_dir, direction, -1))
        fourth = (offset_core(ext_state, direction, -2) - 4.0 * offset_core(ext_state, direction, -1)
                  + 6.0 * offset_core(ext_state, direction, 0) - 4.0 * offset_core(ext_state, direction, 1)
                  + offset_core(ext_state, direction, 2))
        residual_sum = residual_sum - dissipation * fourth
    return residual_sum


def jacobian_term(matrix, sign_flip, velocity, field):
    return beta_coupling * (apply_block(matrix, field) + sign_flip * velocity * field)


def sweep(lead_term, cell_scale, vel_x, vel_y, mat_x, mat_y, sign_flip, west_face, south_face, inverse):
    extent_x = lead_term.shape[1]
    extent_y = lead_term.shape[2]
    row_ids = jnp.arange(extent_x, dtype=jnp.int32)
    col_ids = jnp.arange(extent_y, dtype=jnp.int32)

    def step(state_carry, diag_num):
        prev_x, prev_y = state_carry
        columns = diag_num - row_ids
        is_valid = (columns >= 0) & (columns < extent_y)
        col_clip = jnp.clip(columns, 0, extent_y - 1)
        west_edge = lax.dynamic_index_in_dim(west_face, jnp.clip(diag_num, 0, extent_y - 1), axis=1, keepdims=True)
        from_west = jnp.concatenate([west_edge, prev_x[:, :-1]], axis=1)
        from_south = jnp.where((columns == 0)[None, :, None], south_face, prev_y)
        cell_lead = lead_term[:, row_ids, col_clip]
        scale_cells = cell_scale[row_ids, col_clip]
        fresh_cells = cell_lead - apply_block(inverse, from_west + from_south) / scale_cells
        fresh_cells = jnp.where(is_valid[None, :, None], fresh_cells, 0.0)
        jac_x = jacobian_term(mat_x, sign_flip, vel_x[row_ids, col_clip], fresh_cells)
        jac_y = jacobian_term(mat_y, sign_flip, vel_y[row_ids, col_clip], fresh_cells)
        return (jac_x, jac_y), fresh_cells

    initial = jnp.zeros((lead_term.shape[0], extent_x, lead_term.shape[3]), lead_term.dtype)
    diag_ids = jnp.arange(extent_x + extent_y - 1, dtype=jnp.int32)
    _, diagonals = lax.scan(step, (initial, initial), diag_ids)
    whole_block = diagonals[row_ids[:, None] + col_ids[None, :], :, row_ids[:, None], :]
    return jnp.transpose(whole_block, (2, 0, 1, 3))


def flip_field(array):
    return jnp.flip(array, axis=(array.ndim - 3, array.ndim - 2))


def reference(density, momentum, energy, forcing, coupling, inverse):
    state = jnp.concatenate([density[None], momentum, energy[None]], axis=0)
    padded = jnp.pad(state, ((0, 0), (2, 2), (2, 2), (2, 2)))
    rsd = residual_rhs(padded, forcing)
    vel_x = momentum[0] / density
    vel_y = momentum[1] / density
    vel_z = momentum[2] / density
    cell_scale = 1.0 + vel_x * vel_x + vel_y * vel_y + vel_z * vel_z
    lead_term = apply_block(inverse, rsd) / cell_scale
    extent_x, extent_y, extent_z = density.shape
    zero_west = jnp.zeros((state.shape[0], extent_y, extent_z), jnp.float32)
    zero_south = jnp.zeros((state.shape[0], extent_x, extent_z), jnp.float32)
    lower = sweep(lead_term, cell_scale, vel_x, vel_y, coupling[0], coupling[1], 1.0, zero_west, zero_south, inverse)
    upper = sweep(flip_field(lower), flip_field(cell_scale), flip_field(vel_x), flip_field(vel_y),
                  coupling[0].T, coupling[1].T, -1.0, zero_west, zero_south, inverse)
    return state + flip_field(upper)
```

```python
import functools

import jax
import jax.numpy as jnp
from jax import lax
from jax.experimental import pallas as pl
from jax.experimental.pallas import tpu as pltpu
from jax.sharding import PartitionSpec as P

precision_high = lax.Precision.HIGHEST
beta_coupling = 0.25
dissipation = 0.05


def extended_2(cells, sides, width):
    for axis, dim in sides:
        count = lax.axis_size(axis)
        ends = count - 1
        head = lax.slice_in_dim(cells, 0, width, axis=dim)
        tail = lax.slice_in_dim(cells, cells.shape[dim] - width, cells.shape[dim], axis=dim)
        cells = jnp.concatenate(
            [
                lax.ppermute(tail, axis, [(i, (i + 1) % count) for i in range(ends)]),
                cells,
                lax.ppermute(head, axis, [((i + 1) % count, i) for i in range(ends)]),
            ],
            axis=dim,
        )
    return cells


def from_behind(block, axis, distance):
    devices = range(lax.axis_size(axis))
    route = [(i - distance, i) for i in devices if i - distance in devices]
    return lax.ppermute(block, axis, route)


def apply_block(matrix, field):
    return jnp.einsum("ab,b...->a...", matrix, field, precision=precision_high)


def fluxes(state):
    density_safe = jnp.where(state[0] > 0.1, state[0], 1.0)
    momentum = state[1:4]
    energy = state[4]
    pressure = 0.4 * (energy - 0.5 * jnp.sum(momentum * momentum, axis=0) / density_safe)
    results = []
    for direction in range(3):
        velocity = momentum[direction] / density_safe
        components = [momentum[direction]]
        for component in range(3):
            extra = pressure if component == direction else 0.0
            components.append(momentum[component] * velocity + extra)
        components.append((energy + pressure) * velocity)
        results.append(jnp.stack(components))
    return jnp.stack(results)


def offset_core(array, axis, offset):
    lead_dims = array.ndim - 3
    slicer = [slice(None)] * lead_dims + [slice(2, -2), slice(2, -2), slice(2, -2)]
    length = array.shape[lead_dims + axis]
    slicer[lead_dims + axis] = slice(2 + offset, length - 2 + offset)
    return array[tuple(slicer)]


def residual_rhs(ext_state, ext_flux, forcing):
    residual_sum = forcing
    for direction in range(3):
        flux_dir = ext_flux[direction]
        residual_sum = residual_sum - 0.5 * (
            offset_core(flux_dir, direction, 1) - offset_core(flux_dir, direction, -1)
        )
        fourth = (
            offset_core(ext_state, direction, -2)
            - 4.0 * offset_core(ext_state, direction, -1)
            + 6.0 * offset_core(ext_state, direction, 0)
            - 4.0 * offset_core(ext_state, direction, 1)
            + offset_core(ext_state, direction, 2)
        )
        residual_sum = residual_sum - dissipation * fourth
    return residual_sum


def jacobian_term(matrix, sign_flip, velocity, field):
    return beta_coupling * (apply_block(matrix, field) + sign_flip * velocity * field)


def sweep(
    lead_term, cell_scale, vel_x, vel_y, mat_x, mat_y, sign_flip, west_face, south_face, inverse
):
    extent_x = lead_term.shape[1]
    extent_y = lead_term.shape[2]
    row_ids = jnp.arange(extent_x, dtype=jnp.int32)
    col_ids = jnp.arange(extent_y, dtype=jnp.int32)

    def step(state_carry, diag_num):
        prev_x, prev_y = state_carry
        columns = diag_num - row_ids
        is_valid = (columns >= 0) & (columns < extent_y)
        col_clip = jnp.clip(columns, 0, extent_y - 1)
        west_edge = lax.dynamic_index_in_dim(
            west_face, jnp.clip(diag_num, 0, extent_y - 1), axis=1, keepdims=True
        )
        from_west = jnp.concatenate([west_edge, prev_x[:, :-1]], axis=1)
        from_south = jnp.where((columns == 0)[None, :, None], south_face, prev_y)
        cell_lead = lead_term[:, row_ids, col_clip]
        scale_cells = cell_scale[row_ids, col_clip]
        fresh_cells = cell_lead - apply_block(inverse, from_west + from_south) / scale_cells
        fresh_cells = jnp.where(is_valid[None, :, None], fresh_cells, 0.0)
        jac_x = jacobian_term(mat_x, sign_flip, vel_x[row_ids, col_clip], fresh_cells)
        jac_y = jacobian_term(mat_y, sign_flip, vel_y[row_ids, col_clip], fresh_cells)
        return ((jac_x, jac_y), fresh_cells)

    initial = jnp.zeros((lead_term.shape[0], extent_x, lead_term.shape[3]), lead_term.dtype)
    diag_ids = jnp.arange(extent_x + extent_y - 1, dtype=jnp.int32)
    _, diagonals = lax.scan(step, (initial, initial), diag_ids)
    whole_block = diagonals[row_ids[:, None] + col_ids[None, :], :, row_ids[:, None], :]
    return jnp.transpose(whole_block, (2, 0, 1, 3))


def flip_field(array):
    return jnp.flip(array, axis=(array.ndim - 3, array.ndim - 2))


def wavefront(
    lead_term,
    cell_scale,
    vel_x,
    vel_y,
    mat_x,
    mat_y,
    sign_flip,
    inverse,
    chain_pos,
    blocks,
    send_x,
    send_y,
):
    nvars, extent_x, extent_y, extent_z = lead_term.shape
    block_depth = extent_z // blocks
    sections = blocks + lax.axis_size("gx") + lax.axis_size("gy") - 2

    def section(section_num, state_carry):
        whole_block, west_face, south_face = state_carry
        block_num = section_num - chain_pos
        is_active = (block_num >= 0) & (block_num < blocks)

        def work(current):
            solved = sweep(
                lead_term,
                cell_scale,
                vel_x,
                vel_y,
                mat_x,
                mat_y,
                sign_flip,
                west_face,
                south_face,
                inverse,
            )
            east_out = jacobian_term(mat_x, sign_flip, vel_x[-1], solved[:, -1])
            north_out = jacobian_term(mat_y, sign_flip, vel_y[:, -1], solved[:, :, -1])
            return (solved, east_out, north_out)

        def skip(current):
            return (
                current,
                jnp.zeros((nvars, extent_y, block_depth), jnp.float32),
                jnp.zeros((nvars, extent_x, block_depth), jnp.float32),
            )

        whole_block, east_out, north_out = lax.cond(is_active, work, skip, whole_block)
        return (whole_block, send_x(east_out), send_y(north_out))

    initial = (
        jnp.zeros_like(lead_term),
        jnp.zeros((nvars, extent_y, block_depth), jnp.float32),
        jnp.zeros((nvars, extent_x, block_depth), jnp.float32),
    )
    whole_block, _, _ = lax.fori_loop(0, sections, section, initial)
    return whole_block


def shards(density, momentum, energy, forcing, coupling, inverse):
    state = jnp.concatenate([density[None], momentum, energy[None]], axis=0)
    nvars = state.shape[0]
    z_pad = ((0, 0), (0, 0), (0, 0), (2, 2))
    own_flux = fluxes(state)
    stacked = jnp.concatenate([state, own_flux.reshape((3 * nvars,) + state.shape[1:])], axis=0)
    extended = extended_2(stacked, (("gx", 1), ("gy", 2)), 2)
    extended = jnp.pad(extended, z_pad)
    ext_state = extended[:nvars]
    ext_flux = extended[nvars:].reshape((3, nvars) + extended.shape[1:])
    rsd = residual_rhs(ext_state, ext_flux, forcing)
    vel_x = momentum[0] / density
    vel_y = momentum[1] / density
    vel_z = momentum[2] / density
    cell_scale = 1.0 + vel_x * vel_x + vel_y * vel_y + vel_z * vel_z
    lead_term = apply_block(inverse, rsd) / cell_scale
    blocks = 1
    pos_x = lax.axis_index("gx")
    pos_y = lax.axis_index("gy")
    lower_pos = pos_x + pos_y
    upper_pos = lax.axis_size("gx") - 1 - pos_x + (lax.axis_size("gy") - 1 - pos_y)

    def lower_send_x(face):
        return from_behind(face, "gx", 1)

    def lower_send_y(face):
        return from_behind(face, "gy", 1)

    def upper_send_x(face):
        return from_behind(face, "gx", -1)

    def upper_send_y(face):
        return from_behind(face, "gy", -1)

    lower = wavefront(
        lead_term,
        cell_scale,
        vel_x,
        vel_y,
        coupling[0],
        coupling[1],
        1.0,
        inverse,
        lower_pos,
        blocks,
        lower_send_x,
        lower_send_y,
    )
    upper = wavefront(
        flip_field(lower),
        flip_field(cell_scale),
        flip_field(vel_x),
        flip_field(vel_y),
        coupling[0].T,
        coupling[1].T,
        -1.0,
        inverse,
        upper_pos,
        blocks,
        upper_send_x,
        upper_send_y,
    )
    return state + flip_field(upper)


SKEW = 2
UNROLL = 4


def flux_of(rho, mom, energy, direction):
    safe = jnp.where(rho > 0.1, rho, 1.0)
    inv_rho = 1.0 / safe
    kinetic = mom[0] * mom[0] + mom[1] * mom[1] + mom[2] * mom[2]
    pressure = 0.4 * (energy - 0.5 * kinetic * inv_rho)
    velocity = mom[direction] * inv_rho
    parts = [mom[direction]]
    for component in range(3):
        part = mom[component] * velocity
        parts.append(part + pressure if component == direction else part)
    parts.append((energy + pressure) * velocity)
    return parts


def spread(vector, row):
    return jnp.broadcast_to(vector[row : row + 1, :], vector.shape)


def step_kernel(
    nx_dev,
    ny_dev,
    density,
    momentum,
    energy,
    forcing,
    coupling,
    inverse,
    w_ref,
    ext,
    flux_y,
    pack,
    out_a,
    in_a,
    grid_a,
    grid_b,
    out_b,
    in_b,
    coef,
    halo_send,
    halo_recv,
    a_send,
    a_recv,
    b_send,
    b_recv,
    own_sem,
):
    devices = nx_dev * ny_dev
    gx = lax.axis_index("gx")
    gy = lax.axis_index("gy")
    me = gy * nx_dev + gx
    mesh_id = pl.DeviceIdType.MESH

    def place(slot):
        return (lax.rem(slot, nx_dev), lax.div(slot, nx_dev))

    def other(offset):
        return lax.rem(me + offset, devices)

    barrier = pltpu.get_barrier_semaphore()

    @pl.loop(1, devices)
    def _(offset):
        pl.semaphore_signal(barrier, inc=1, device_id=place(other(offset)), device_id_type=mesh_id)

    ext[0, 2:4, 8:24, :] = density[...]
    for component in range(3):
        ext[1 + component, 2:4, 8:24, :] = momentum[component]
    ext[4, 2:4, 8:24, :] = energy[...]

    @pl.when(gx == 0)
    def _():
        ext[:, 0:2, 8:24, :] = jnp.zeros((5, 2, 16, 128), jnp.float32)

    @pl.when(gx == nx_dev - 1)
    def _():
        ext[:, 4:6, 8:24, :] = jnp.zeros((5, 2, 16, 128), jnp.float32)

    @pl.when(gy == 0)
    def _():
        ext[:, 2:4, 0:8, :] = jnp.zeros((5, 2, 8, 128), jnp.float32)

    @pl.when(gy == ny_dev - 1)
    def _():
        ext[:, 2:4, 24:32, :] = jnp.zeros((5, 2, 8, 128), jnp.float32)

    pl.semaphore_wait(barrier, devices - 1)

    block = ext.at[:, 2:4, 8:24, :]
    to_east = pltpu.make_async_remote_copy(
        block, ext.at[:, 0:2, 8:24, :], halo_send.at[0], halo_recv.at[0], (gx + 1, gy), mesh_id
    )
    to_west = pltpu.make_async_remote_copy(
        block, ext.at[:, 4:6, 8:24, :], halo_send.at[1], halo_recv.at[1], (gx - 1, gy), mesh_id
    )
    to_north = pltpu.make_async_remote_copy(
        ext.at[:, 2:4, 16:24, :],
        ext.at[:, 2:4, 0:8, :],
        halo_send.at[2],
        halo_recv.at[2],
        (gx, gy + 1),
        mesh_id,
    )
    to_south = pltpu.make_async_remote_copy(
        ext.at[:, 2:4, 8:16, :],
        ext.at[:, 2:4, 24:32, :],
        halo_send.at[3],
        halo_recv.at[3],
        (gx, gy - 1),
        mesh_id,
    )
    sides = (
        (to_east, gx < nx_dev - 1, gx > 0),
        (to_west, gx > 0, gx < nx_dev - 1),
        (to_north, gy < ny_dev - 1, gy > 0),
        (to_south, gy > 0, gy < ny_dev - 1),
    )
    for copy, sends, _ in sides:
        pl.when(sends)(copy.start)

    row_id = lax.broadcasted_iota(jnp.int32, (8, 128), 0)
    inv_cols = []
    for c in range(5):
        column = jnp.zeros((8, 128), jnp.float32)
        for a in range(5):
            column = jnp.where(row_id == a, 0.25 * inverse[a, c], column)
        inv_cols.append(column)
        coef[4, c] = column
    for d in range(2):
        for b in range(5):
            lower = inv_cols[0] * coupling[d, 0, b]
            upper = inv_cols[0] * coupling[d, b, 0]
            for c in range(1, 5):
                lower = lower + inv_cols[c] * coupling[d, c, b]
                upper = upper + inv_cols[c] * coupling[d, b, c]
            coef[d, b] = lower
            coef[2 + d, b] = upper
    grid_a[...] = jnp.zeros(grid_a.shape, jnp.float32)
    grid_b[...] = jnp.zeros(grid_b.shape, jnp.float32)

    rho = density[...]
    mom = [momentum[c] for c in range(3)]
    en = energy[...]
    inv_rho = 1.0 / rho
    vel = [m * inv_rho for m in mom]
    inv_scale = 1.0 / (1.0 + vel[0] * vel[0] + vel[1] * vel[1] + vel[2] * vel[2])
    own = [rho] + mom + [en]
    flux_z = flux_of(rho, mom, en, 2)
    lane3 = lax.broadcasted_iota(jnp.int32, (2, 16, 128), 2)

    def from_z(field, offset):
        moved = pltpu.roll(field.reshape(32, 128), (-offset) % 128, 1).reshape(2, 16, 128)
        inside = (lane3 < 128 - offset) if offset > 0 else (lane3 >= -offset)
        return jnp.where(inside, moved, 0.0)

    rsd = []
    for f in range(5):
        total = forcing[f] - (18.0 * dissipation) * own[f]
        total = total + from_z(4.0 * dissipation * own[f] - 0.5 * flux_z[f], 1)
        total = total + from_z(4.0 * dissipation * own[f] + 0.5 * flux_z[f], -1)
        total = total - dissipation * (from_z(own[f], 2) + from_z(own[f], -2))
        rsd.append(total)

    for copy, _, receives in sides:
        pl.when(receives)(copy.wait_recv)

    wide = [ext[f, 1:5, 8:24, :] for f in range(5)]
    flux_x = flux_of(wide[0], wide[1:4], wide[4], 0)
    tall = [ext[f, 2:4, :, :] for f in range(5)]
    for f, part in enumerate(flux_of(tall[0], tall[1:4], tall[4], 1)):
        flux_y[f] = part
    for f in range(5):
        total = rsd[f] - 0.5 * (flux_x[f][2:4] - flux_x[f][0:2])
        total = total - 0.5 * (flux_y[f, :, 9:25, :] - flux_y[f, :, 7:23, :])
        near = (wide[f][0:2] + wide[f][2:4]) + (ext[f, 2:4, 7:23, :] + ext[f, 2:4, 9:25, :])
        far = (ext[f, 0:2, 8:24, :] + ext[f, 4:6, 8:24, :]) + (
            ext[f, 2:4, 6:22, :] + ext[f, 2:4, 10:26, :]
        )
        rsd[f] = total + dissipation * (4.0 * near - far)

    fields = []
    for a in range(5):
        total = inverse[a, 0] * rsd[0]
        for b in range(1, 5):
            total = total + inverse[a, b] * rsd[b]
        fields.append(total * inv_scale)
    fields += [vel[0], vel[1], inv_scale]

    for xl in range(2):
        for f in range(8):
            pack[pl.ds(xl * 128 + f, 16, stride=8), :] = fields[f][xl]
        turned = pack[xl * 128 : (xl + 1) * 128, :].T
        for part in range(4):
            out_a[pl.ds(xl * 4 + part, 32, stride=8), :] = turned[part * 32 : (part + 1) * 32]

    def tile(ref, slot):
        return ref.at[pl.ds(pl.multiple_of(slot * 8, 8), 8), :]

    def exchange(source, target, send, recv):
        def to_slot(offset):
            slot = other(offset)
            return pltpu.make_async_remote_copy(
                tile(source, slot), tile(target, me), send.at[slot], recv.at[me], place(slot), mesh_id
            )

        def from_slot(offset):
            slot = other(offset)
            return pltpu.make_async_remote_copy(
                tile(source, slot), tile(target, slot), send.at[slot], recv.at[slot], place(slot), mesh_id
            )

        pl.loop(1, devices)(lambda offset: to_slot(offset).start())
        mine = pltpu.make_async_copy(tile(source, me), tile(target, me), own_sem)
        mine.start()
        mine.wait()
        pl.loop(1, devices)(lambda offset: from_slot(offset).wait_recv())

        return lambda: pl.loop(1, devices)(lambda offset: to_slot(offset).wait_send())

    finish_a = exchange(out_a, in_a, a_send, a_recv)

    lane = lax.broadcasted_iota(jnp.int32, (128, 128), 1)
    low = lane < 64
    front = 8 * SKEW
    for pair in range(ny_dev // 2):
        turned = in_a[pair * 128 : (pair + 1) * 128, :].T
        first = front + pair * 32
        grid_a[first : first + 16] = jnp.where(low, turned, 0.0).reshape(16, 8, 128)
        turned = pltpu.roll(turned, 64, 1)
        grid_a[first + 16 : first + 32] = jnp.where(low, turned, 0.0).reshape(16, 8, 128)

    extent_y = 16 * ny_dev
    lane_x = lax.broadcasted_iota(jnp.int32, (1, 8, 128), 2) // 4
    buffers = (grid_a, grid_b)
    for bit in range(4):
        source, target = buffers[bit % 2], buffers[1 - bit % 2]
        shift = SKEW << bit
        rows = extent_y + SKEW * ((2 << bit) - 1)
        odd = (lane_x // (1 << bit)) % 2 == 1
        target[front : front + rows] = jnp.where(
            odd, source[front - shift : front - shift + rows], source[front : front + rows]
        )

    steps = extent_y + 15 * SKEW
    steps = -(-steps // UNROLL) * UNROLL
    zero = jnp.zeros((8, 128), jnp.float32)

    def run_sweep(first_coef, sign, roll_by, row_of):
        mat_x = [coef[first_coef, b] for b in range(5)]
        mat_y = [coef[first_coef + 1, b] for b in range(5)]
        mat_i = [coef[4, b] for b in range(5)]

        def advance(index, carry):
            south, queue = carry[0], list(carry[1:])
            for inner in range(UNROLL):
                row = row_of(index * UNROLL + inner)
                cells = grid_a[row]
                cells = cells - spread(cells, 7) * (south + queue.pop(0))
                grid_a[row] = cells
                speed_x = sign * spread(cells, 5)
                speed_y = sign * spread(cells, 6)
                values = [spread(cells, b) for b in range(5)]
                terms = [(mat_y[b] + speed_y * mat_i[b]) * values[b] for b in range(5)]
                south = ((terms[0] + terms[1]) + (terms[2] + terms[3])) + terms[4]
                terms = [(mat_x[b] + speed_x * mat_i[b]) * values[b] for b in range(5)]
                west = ((terms[0] + terms[1]) + (terms[2] + terms[3])) + terms[4]
                queue.append(pltpu.roll(west, roll_by, 1))
            return (south, *queue)

        lax.fori_loop(0, steps // UNROLL, advance, (zero,) * (1 + SKEW))

    run_sweep(0, 1.0, 4, lambda step: front + step)
    run_sweep(2, -1.0, 124, lambda step: front + steps - 1 - step)

    for turn, bit in enumerate((3, 2, 1, 0)):
        source, target = buffers[turn % 2], buffers[1 - turn % 2]
        shift = SKEW << bit
        rows = extent_y + SKEW * ((1 << bit) - 1)
        odd = (lane_x // (1 << bit)) % 2 == 1
        target[front : front + rows] = jnp.where(
            odd, source[front + shift : front + shift + rows], source[front : front + rows]
        )

    for pair in range(ny_dev // 2):
        first = front + pair * 32
        left = grid_a[first : first + 16].reshape(128, 128)
        right = pltpu.roll(grid_a[first + 16 : first + 32].reshape(128, 128), 64, 1)
        out_b[pair * 128 : (pair + 1) * 128, :] = jnp.where(low, left, right).T

    finish_b = exchange(out_b, in_b, b_send, b_recv)

    for xl in range(2):
        planes = [in_b[pl.ds(xl * 4 + part, 32, stride=8), :] for part in range(4)]
        pack[xl * 128 : (xl + 1) * 128, :] = jnp.concatenate(planes, axis=0).T
        for f in range(5):
            w_ref[f, xl] = pack[pl.ds(xl * 128 + f, 16, stride=8), :]

    for copy, sends, _ in sides:
        pl.when(sends)(copy.wait_send)
    finish_a()
    finish_b()


def kernel_shards(nx_dev, ny_dev, density, momentum, energy, forcing, coupling, inverse):
    devices = nx_dev * ny_dev
    grid_rows = 8 * SKEW + 16 * ny_dev + 15 * SKEW + UNROLL
    vmem = pl.BlockSpec(memory_space=pltpu.VMEM)
    smem = pl.BlockSpec(memory_space=pltpu.SMEM)
    change = pl.pallas_call(
        functools.partial(step_kernel, nx_dev, ny_dev),
        out_shape=jax.ShapeDtypeStruct((5, 2, 16, 128), jnp.float32),
        in_specs=[vmem] * 4 + [smem] * 2,
        out_specs=vmem,
        scratch_shapes=[
            pltpu.VMEM((5, 6, 32, 128), jnp.float32),
            pltpu.VMEM((5, 2, 32, 128), jnp.float32),
            pltpu.VMEM((256, 128), jnp.float32),
            pltpu.VMEM((8 * devices, 128), jnp.float32),
            pltpu.VMEM((8 * devices, 128), jnp.float32),
            pltpu.VMEM((grid_rows, 8, 128), jnp.float32),
            pltpu.VMEM((grid_rows, 8, 128), jnp.float32),
            pltpu.VMEM((8 * devices, 128), jnp.float32),
            pltpu.VMEM((8 * devices, 128), jnp.float32),
            pltpu.VMEM((5, 5, 8, 128), jnp.float32),
            pltpu.SemaphoreType.DMA((4,)),
            pltpu.SemaphoreType.DMA((4,)),
            pltpu.SemaphoreType.DMA((devices,)),
            pltpu.SemaphoreType.DMA((devices,)),
            pltpu.SemaphoreType.DMA((devices,)),
            pltpu.SemaphoreType.DMA((devices,)),
            pltpu.SemaphoreType.DMA,
        ],
        compiler_params=pltpu.CompilerParams(
            collective_id=0, has_side_effects=True, vmem_limit_bytes=32 * 1024 * 1024
        ),
        name="lu_step",
    )(density, momentum, energy, forcing, coupling, inverse)
    state = jnp.concatenate([density[None], momentum, energy[None]], axis=0)
    return state + change


def solution(mesh):
    placed = (
        P("gx", "gy", None),
        P(None, "gx", "gy", None),
        P("gx", "gy", None),
        P(None, "gx", "gy", None),
        P(),
        P(),
    )
    nx_dev, ny_dev = mesh.shape["gx"], mesh.shape["gy"]

    def local(*args):
        if args[0].shape == (2, 16, 128) and (nx_dev, ny_dev) == (8, 4):
            return kernel_shards(nx_dev, ny_dev, *args)
        return shards(*args)

    return jax.shard_map(
        local, mesh=mesh, in_specs=placed, out_specs=P(None, "gx", "gy", None), check_vma=False
    )
```

```python
import functools

import jax
import jax.numpy as jnp
from jax import lax
from jax.experimental import pallas as pl
from jax.experimental.pallas import tpu as pltpu
from jax.sharding import PartitionSpec as P

precision_high = lax.Precision.HIGHEST
beta_coupling = 0.25
dissipation = 0.05


def extended_2(cells, sides, width):
    for axis, dim in sides:
        count = lax.axis_size(axis)
        ends = count - 1
        head = lax.slice_in_dim(cells, 0, width, axis=dim)
        tail = lax.slice_in_dim(cells, cells.shape[dim] - width, cells.shape[dim], axis=dim)
        cells = jnp.concatenate(
            [
                lax.ppermute(tail, axis, [(i, (i + 1) % count) for i in range(ends)]),
                cells,
                lax.ppermute(head, axis, [((i + 1) % count, i) for i in range(ends)]),
            ],
            axis=dim,
        )
    return cells


def from_behind(block, axis, distance):
    devices = range(lax.axis_size(axis))
    route = [(i - distance, i) for i in devices if i - distance in devices]
    return lax.ppermute(block, axis, route)


def apply_block(matrix, field):
    return jnp.einsum("ab,b...->a...", matrix, field, precision=precision_high)


def fluxes(state):
    density_safe = jnp.where(state[0] > 0.1, state[0], 1.0)
    momentum = state[1:4]
    energy = state[4]
    pressure = 0.4 * (energy - 0.5 * jnp.sum(momentum * momentum, axis=0) / density_safe)
    results = []
    for direction in range(3):
        velocity = momentum[direction] / density_safe
        components = [momentum[direction]]
        for component in range(3):
            extra = pressure if component == direction else 0.0
            components.append(momentum[component] * velocity + extra)
        components.append((energy + pressure) * velocity)
        results.append(jnp.stack(components))
    return jnp.stack(results)


def offset_core(array, axis, offset):
    lead_dims = array.ndim - 3
    slicer = [slice(None)] * lead_dims + [slice(2, -2), slice(2, -2), slice(2, -2)]
    length = array.shape[lead_dims + axis]
    slicer[lead_dims + axis] = slice(2 + offset, length - 2 + offset)
    return array[tuple(slicer)]


def residual_rhs(ext_state, ext_flux, forcing):
    residual_sum = forcing
    for direction in range(3):
        flux_dir = ext_flux[direction]
        residual_sum = residual_sum - 0.5 * (
            offset_core(flux_dir, direction, 1) - offset_core(flux_dir, direction, -1)
        )
        fourth = (
            offset_core(ext_state, direction, -2)
            - 4.0 * offset_core(ext_state, direction, -1)
            + 6.0 * offset_core(ext_state, direction, 0)
            - 4.0 * offset_core(ext_state, direction, 1)
            + offset_core(ext_state, direction, 2)
        )
        residual_sum = residual_sum - dissipation * fourth
    return residual_sum


def jacobian_term(matrix, sign_flip, velocity, field):
    return beta_coupling * (apply_block(matrix, field) + sign_flip * velocity * field)


def sweep(
    lead_term, cell_scale, vel_x, vel_y, mat_x, mat_y, sign_flip, west_face, south_face, inverse
):
    extent_x = lead_term.shape[1]
    extent_y = lead_term.shape[2]
    row_ids = jnp.arange(extent_x, dtype=jnp.int32)
    col_ids = jnp.arange(extent_y, dtype=jnp.int32)

    def step(state_carry, diag_num):
        prev_x, prev_y = state_carry
        columns = diag_num - row_ids
        is_valid = (columns >= 0) & (columns < extent_y)
        col_clip = jnp.clip(columns, 0, extent_y - 1)
        west_edge = lax.dynamic_index_in_dim(
            west_face, jnp.clip(diag_num, 0, extent_y - 1), axis=1, keepdims=True
        )
        from_west = jnp.concatenate([west_edge, prev_x[:, :-1]], axis=1)
        from_south = jnp.where((columns == 0)[None, :, None], south_face, prev_y)
        cell_lead = lead_term[:, row_ids, col_clip]
        scale_cells = cell_scale[row_ids, col_clip]
        fresh_cells = cell_lead - apply_block(inverse, from_west + from_south) / scale_cells
        fresh_cells = jnp.where(is_valid[None, :, None], fresh_cells, 0.0)
        jac_x = jacobian_term(mat_x, sign_flip, vel_x[row_ids, col_clip], fresh_cells)
        jac_y = jacobian_term(mat_y, sign_flip, vel_y[row_ids, col_clip], fresh_cells)
        return ((jac_x, jac_y), fresh_cells)

    initial = jnp.zeros((lead_term.shape[0], extent_x, lead_term.shape[3]), lead_term.dtype)
    diag_ids = jnp.arange(extent_x + extent_y - 1, dtype=jnp.int32)
    _, diagonals = lax.scan(step, (initial, initial), diag_ids)
    whole_block = diagonals[row_ids[:, None] + col_ids[None, :], :, row_ids[:, None], :]
    return jnp.transpose(whole_block, (2, 0, 1, 3))


def flip_field(array):
    return jnp.flip(array, axis=(array.ndim - 3, array.ndim - 2))


def wavefront(
    lead_term,
    cell_scale,
    vel_x,
    vel_y,
    mat_x,
    mat_y,
    sign_flip,
    inverse,
    chain_pos,
    blocks,
    send_x,
    send_y,
):
    nvars, extent_x, extent_y, extent_z = lead_term.shape
    block_depth = extent_z // blocks
    sections = blocks + lax.axis_size("gx") + lax.axis_size("gy") - 2

    def section(section_num, state_carry):
        whole_block, west_face, south_face = state_carry
        block_num = section_num - chain_pos
        is_active = (block_num >= 0) & (block_num < blocks)

        def work(current):
            solved = sweep(
                lead_term,
                cell_scale,
                vel_x,
                vel_y,
                mat_x,
                mat_y,
                sign_flip,
                west_face,
                south_face,
                inverse,
            )
            east_out = jacobian_term(mat_x, sign_flip, vel_x[-1], solved[:, -1])
            north_out = jacobian_term(mat_y, sign_flip, vel_y[:, -1], solved[:, :, -1])
            return (solved, east_out, north_out)

        def skip(current):
            return (
                current,
                jnp.zeros((nvars, extent_y, block_depth), jnp.float32),
                jnp.zeros((nvars, extent_x, block_depth), jnp.float32),
            )

        whole_block, east_out, north_out = lax.cond(is_active, work, skip, whole_block)
        return (whole_block, send_x(east_out), send_y(north_out))

    initial = (
        jnp.zeros_like(lead_term),
        jnp.zeros((nvars, extent_y, block_depth), jnp.float32),
        jnp.zeros((nvars, extent_x, block_depth), jnp.float32),
    )
    whole_block, _, _ = lax.fori_loop(0, sections, section, initial)
    return whole_block


def shards(density, momentum, energy, forcing, coupling, inverse):
    state = jnp.concatenate([density[None], momentum, energy[None]], axis=0)
    nvars = state.shape[0]
    z_pad = ((0, 0), (0, 0), (0, 0), (2, 2))
    own_flux = fluxes(state)
    stacked = jnp.concatenate([state, own_flux.reshape((3 * nvars,) + state.shape[1:])], axis=0)
    extended = extended_2(stacked, (("gx", 1), ("gy", 2)), 2)
    extended = jnp.pad(extended, z_pad)
    ext_state = extended[:nvars]
    ext_flux = extended[nvars:].reshape((3, nvars) + extended.shape[1:])
    rsd = residual_rhs(ext_state, ext_flux, forcing)
    vel_x = momentum[0] / density
    vel_y = momentum[1] / density
    vel_z = momentum[2] / density
    cell_scale = 1.0 + vel_x * vel_x + vel_y * vel_y + vel_z * vel_z
    lead_term = apply_block(inverse, rsd) / cell_scale
    blocks = 1
    pos_x = lax.axis_index("gx")
    pos_y = lax.axis_index("gy")
    lower_pos = pos_x + pos_y
    upper_pos = lax.axis_size("gx") - 1 - pos_x + (lax.axis_size("gy") - 1 - pos_y)

    def lower_send_x(face):
        return from_behind(face, "gx", 1)

    def lower_send_y(face):
        return from_behind(face, "gy", 1)

    def upper_send_x(face):
        return from_behind(face, "gx", -1)

    def upper_send_y(face):
        return from_behind(face, "gy", -1)

    lower = wavefront(
        lead_term,
        cell_scale,
        vel_x,
        vel_y,
        coupling[0],
        coupling[1],
        1.0,
        inverse,
        lower_pos,
        blocks,
        lower_send_x,
        lower_send_y,
    )
    upper = wavefront(
        flip_field(lower),
        flip_field(cell_scale),
        flip_field(vel_x),
        flip_field(vel_y),
        coupling[0].T,
        coupling[1].T,
        -1.0,
        inverse,
        upper_pos,
        blocks,
        upper_send_x,
        upper_send_y,
    )
    return state + flip_field(upper)


SKEW = 4
UNROLL = 8


def flux_of(rho, mom, energy, direction):
    safe = jnp.where(rho > 0.1, rho, 1.0)
    inv_rho = 1.0 / safe
    kinetic = mom[0] * mom[0] + mom[1] * mom[1] + mom[2] * mom[2]
    pressure = 0.4 * (energy - 0.5 * kinetic * inv_rho)
    velocity = mom[direction] * inv_rho
    parts = [mom[direction]]
    for component in range(3):
        part = mom[component] * velocity
        parts.append(part + pressure if component == direction else part)
    parts.append((energy + pressure) * velocity)
    return parts


def spread(vector, row):
    return jnp.broadcast_to(vector[row : row + 1, :], vector.shape)


def step_kernel(
    nx_dev,
    ny_dev,
    density_hbm,
    momentum_hbm,
    energy_hbm,
    forcing_hbm,
    coupling_hbm,
    inverse_hbm,
    w_ref,
    ext,
    forcing,
    coupling,
    inverse,
    flux_y,
    pack,
    out_a,
    in_a,
    grid_a,
    grid_b,
    out_b,
    in_b,
    coef,
    halo_send,
    halo_recv,
    a_send,
    a_recv,
    b_send,
    b_recv,
    own_sem,
    load_sem,
):
    devices = nx_dev * ny_dev
    gx = lax.axis_index("gx")
    gy = lax.axis_index("gy")
    me = gy * nx_dev + gx
    mesh_id = pl.DeviceIdType.MESH

    def place(slot):
        return (lax.rem(slot, nx_dev), lax.div(slot, nx_dev))

    def other(offset):
        return lax.rem(me + offset, devices)

    middle = (slice(2, 4), slice(8, 24), slice(None))
    loads = [
        pltpu.make_async_copy(source, target, load_sem.at[number])
        for number, (source, target) in enumerate(
            (
                (density_hbm, ext.at[(0,) + middle]),
                (momentum_hbm, ext.at[(slice(1, 4),) + middle]),
                (energy_hbm, ext.at[(4,) + middle]),
                (forcing_hbm, forcing),
                (coupling_hbm, coupling),
                (inverse_hbm, inverse),
            )
        )
    ]
    for load in loads:
        load.start()

    barrier = pltpu.get_barrier_semaphore()

    @pl.loop(1, devices)
    def _(offset):
        pl.semaphore_signal(barrier, inc=1, device_id=place(other(offset)), device_id_type=mesh_id)

    @pl.when(gx == 0)
    def _():
        ext[:, 0:2, 8:24, :] = jnp.zeros((5, 2, 16, 128), jnp.float32)

    @pl.when(gx == nx_dev - 1)
    def _():
        ext[:, 4:6, 8:24, :] = jnp.zeros((5, 2, 16, 128), jnp.float32)

    @pl.when(gy == 0)
    def _():
        ext[:, 2:4, 0:8, :] = jnp.zeros((5, 2, 8, 128), jnp.float32)

    @pl.when(gy == ny_dev - 1)
    def _():
        ext[:, 2:4, 24:32, :] = jnp.zeros((5, 2, 8, 128), jnp.float32)

    loads[4].wait()
    loads[5].wait()
    row_id = lax.broadcasted_iota(jnp.int32, (8, 128), 0)
    inv_cols = []
    for c in range(5):
        column = jnp.zeros((8, 128), jnp.float32)
        for a in range(5):
            column = jnp.where(row_id == a, 0.25 * inverse[a, c], column)
        inv_cols.append(column)
        coef[4, c] = column
    for d in range(2):
        for b in range(5):
            lower = inv_cols[0] * coupling[0, d, b]
            upper = inv_cols[0] * coupling[b, d, 0]
            for c in range(1, 5):
                lower = lower + inv_cols[c] * coupling[c, d, b]
                upper = upper + inv_cols[c] * coupling[b, d, c]
            coef[d, b] = lower
            coef[2 + d, b] = upper
    grid_a[...] = jnp.zeros(grid_a.shape, jnp.float32)
    grid_b[...] = jnp.zeros(grid_b.shape, jnp.float32)

    for load in loads[:3]:
        load.wait()
    pl.semaphore_wait(barrier, devices - 1)

    block = ext.at[:, 2:4, 8:24, :]
    to_east = pltpu.make_async_remote_copy(
        block, ext.at[:, 0:2, 8:24, :], halo_send.at[0], halo_recv.at[0], (gx + 1, gy), mesh_id
    )
    to_west = pltpu.make_async_remote_copy(
        block, ext.at[:, 4:6, 8:24, :], halo_send.at[1], halo_recv.at[1], (gx - 1, gy), mesh_id
    )
    to_north = pltpu.make_async_remote_copy(
        ext.at[:, 2:4, 16:24, :],
        ext.at[:, 2:4, 0:8, :],
        halo_send.at[2],
        halo_recv.at[2],
        (gx, gy + 1),
        mesh_id,
    )
    to_south = pltpu.make_async_remote_copy(
        ext.at[:, 2:4, 8:16, :],
        ext.at[:, 2:4, 24:32, :],
        halo_send.at[3],
        halo_recv.at[3],
        (gx, gy - 1),
        mesh_id,
    )
    sides = (
        (to_east, gx < nx_dev - 1, gx > 0),
        (to_west, gx > 0, gx < nx_dev - 1),
        (to_north, gy < ny_dev - 1, gy > 0),
        (to_south, gy > 0, gy < ny_dev - 1),
    )
    for copy, sends, _ in sides:
        pl.when(sends)(copy.start)

    loads[3].wait()
    rho, *mom, en = [ext[f, 2:4, 8:24, :] for f in range(5)]
    inv_rho = 1.0 / rho
    vel = [m * inv_rho for m in mom]
    inv_scale = 1.0 / (1.0 + vel[0] * vel[0] + vel[1] * vel[1] + vel[2] * vel[2])
    own = [rho] + mom + [en]
    flux_z = flux_of(rho, mom, en, 2)
    lane3 = lax.broadcasted_iota(jnp.int32, (2, 16, 128), 2)

    def from_z(field, offset):
        moved = pltpu.roll(field.reshape(32, 128), (-offset) % 128, 1).reshape(2, 16, 128)
        inside = (lane3 < 128 - offset) if offset > 0 else (lane3 >= -offset)
        return jnp.where(inside, moved, 0.0)

    rsd = []
    for f in range(5):
        total = forcing[f] - (18.0 * dissipation) * own[f]
        total = total + from_z(4.0 * dissipation * own[f] - 0.5 * flux_z[f], 1)
        total = total + from_z(4.0 * dissipation * own[f] + 0.5 * flux_z[f], -1)
        total = total - dissipation * (from_z(own[f], 2) + from_z(own[f], -2))
        rsd.append(total)

    for copy, _, receives in sides:
        pl.when(receives)(copy.wait_recv)

    wide = [ext[f, 1:5, 8:24, :] for f in range(5)]
    flux_x = flux_of(wide[0], wide[1:4], wide[4], 0)
    tall = [ext[f, 2:4, :, :] for f in range(5)]
    for f, part in enumerate(flux_of(tall[0], tall[1:4], tall[4], 1)):
        flux_y[f] = part
    for f in range(5):
        total = rsd[f] - 0.5 * (flux_x[f][2:4] - flux_x[f][0:2])
        total = total - 0.5 * (flux_y[f, :, 9:25, :] - flux_y[f, :, 7:23, :])
        near = (wide[f][0:2] + wide[f][2:4]) + (ext[f, 2:4, 7:23, :] + ext[f, 2:4, 9:25, :])
        far = (ext[f, 0:2, 8:24, :] + ext[f, 4:6, 8:24, :]) + (
            ext[f, 2:4, 6:22, :] + ext[f, 2:4, 10:26, :]
        )
        rsd[f] = total + dissipation * (4.0 * near - far)

    fields = []
    for a in range(5):
        total = inverse[a, 0] * rsd[0]
        for b in range(1, 5):
            total = total + inverse[a, b] * rsd[b]
        fields.append(total * inv_scale)
    fields += [vel[0], vel[1], inv_scale]

    for xl in range(2):
        for f in range(8):
            pack[pl.ds(xl * 128 + f, 16, stride=8), :] = fields[f][xl]
        turned = pack[xl * 128 : (xl + 1) * 128, :].T
        for part in range(4):
            out_a[pl.ds(xl * 4 + part, 32, stride=8), :] = turned[part * 32 : (part + 1) * 32]

    def tile(ref, slot):
        return ref.at[pl.ds(pl.multiple_of(slot * 8, 8), 8), :]

    def exchange(source, target, send, recv):
        @pl.loop(1, devices)
        def _(offset):
            slot = other(offset)
            pltpu.make_async_remote_copy(
                tile(source, slot), tile(target, me), send, recv, place(slot), mesh_id
            ).start()

        mine = pltpu.make_async_copy(tile(source, me), tile(target, me), own_sem)
        mine.start()
        mine.wait()
        rows = pl.ds(0, 8 * (devices - 1))
        whole = pltpu.make_async_remote_copy(
            source.at[rows, :], target.at[rows, :], send, recv, place(other(1)), mesh_id
        )
        whole.wait_recv()
        return whole.wait_send

    finish_a = exchange(out_a, in_a, a_send, a_recv)

    lane = lax.broadcasted_iota(jnp.int32, (128, 128), 1)
    low = lane < 64
    front = 8 * SKEW
    for pair in range(ny_dev // 2):
        turned = in_a[pair * 128 : (pair + 1) * 128, :].T
        first = front + pair * 32
        grid_a[first : first + 16] = jnp.where(low, turned, 0.0).reshape(16, 8, 128)
        turned = pltpu.roll(turned, 64, 1)
        grid_a[first + 16 : first + 32] = jnp.where(low, turned, 0.0).reshape(16, 8, 128)

    extent_y = 16 * ny_dev
    lane_x = lax.broadcasted_iota(jnp.int32, (1, 8, 128), 2) // 4
    buffers = (grid_a, grid_b)
    for bit in range(4):
        source, target = buffers[bit % 2], buffers[1 - bit % 2]
        shift = SKEW << bit
        rows = extent_y + SKEW * ((2 << bit) - 1)
        odd = (lane_x // (1 << bit)) % 2 == 1
        target[front : front + rows] = jnp.where(
            odd, source[front - shift : front - shift + rows], source[front : front + rows]
        )

    steps = extent_y + 15 * SKEW
    steps = -(-steps // UNROLL) * UNROLL
    zero = jnp.zeros((8, 128), jnp.float32)

    def run_sweep(first_coef, sign, roll_by, row_of):
        mat_x = [coef[first_coef, b] for b in range(5)]
        mat_y = [coef[first_coef + 1, b] for b in range(5)]
        mat_i = [coef[4, b] for b in range(5)]

        def advance(index, carry):
            first, second, third, *queue = carry
            for inner in range(UNROLL):
                row = row_of(index * UNROLL + inner)
                after = spread(grid_a[row_of(index * UNROLL + inner + 1)], 7)
                cells = grid_a[row]
                speed_x = sign * spread(cells, 5)
                speed_y = sign * spread(cells, 6)
                cells = cells - spread(cells, 7) * pltpu.roll(queue.pop(0), roll_by, 1)
                cells = ((cells - first) - second) - third
                grid_a[row] = cells
                values = [spread(cells, b) for b in range(5)]
                terms = [((mat_y[b] + speed_y * mat_i[b]) * after) * values[b] for b in range(5)]
                first, second, third = terms[0], terms[1] + terms[2], terms[3] + terms[4]
                terms = [(mat_x[b] + speed_x * mat_i[b]) * values[b] for b in range(5)]
                queue.append(((terms[0] + terms[1]) + (terms[2] + terms[3])) + terms[4])
            return (first, second, third, *queue)

        lax.fori_loop(0, steps // UNROLL, advance, (zero,) * (3 + SKEW))

    run_sweep(0, 1.0, 4, lambda step: front + step)
    run_sweep(2, -1.0, 124, lambda step: front + steps - 1 - step)

    for turn, bit in enumerate((3, 2, 1, 0)):
        source, target = buffers[turn % 2], buffers[1 - turn % 2]
        shift = SKEW << bit
        rows = extent_y + SKEW * ((1 << bit) - 1)
        odd = (lane_x // (1 << bit)) % 2 == 1
        target[front : front + rows] = jnp.where(
            odd, source[front + shift : front + shift + rows], source[front : front + rows]
        )

    for pair in range(ny_dev // 2):
        first = front + pair * 32
        left = grid_a[first : first + 16].reshape(128, 128)
        right = pltpu.roll(grid_a[first + 16 : first + 32].reshape(128, 128), 64, 1)
        out_b[pair * 128 : (pair + 1) * 128, :] = jnp.where(low, left, right).T

    finish_b = exchange(out_b, in_b, b_send, b_recv)

    for xl in range(2):
        planes = [in_b[pl.ds(xl * 4 + part, 32, stride=8), :] for part in range(4)]
        pack[xl * 128 : (xl + 1) * 128, :] = jnp.concatenate(planes, axis=0).T
        for f in range(5):
            w_ref[f, xl] = pack[pl.ds(xl * 128 + f, 16, stride=8), :]

    for copy, sends, _ in sides:
        pl.when(sends)(copy.wait_send)
    finish_a()
    finish_b()


def kernel_shards(nx_dev, ny_dev, density, momentum, energy, forcing, coupling, inverse):
    devices = nx_dev * ny_dev
    grid_rows = 8 * SKEW + 16 * ny_dev + 15 * SKEW + UNROLL
    vmem = pl.BlockSpec(memory_space=pltpu.VMEM)
    change = pl.pallas_call(
        functools.partial(step_kernel, nx_dev, ny_dev),
        out_shape=jax.ShapeDtypeStruct((5, 2, 16, 128), jnp.float32),
        in_specs=[pl.BlockSpec(memory_space=pltpu.HBM)] * 6,
        out_specs=vmem,
        scratch_shapes=[
            pltpu.VMEM((5, 6, 32, 128), jnp.float32),
            pltpu.VMEM((5, 2, 16, 128), jnp.float32),
            pltpu.SMEM((5, 2, 5), jnp.float32),
            pltpu.SMEM((5, 5), jnp.float32),
            pltpu.VMEM((5, 2, 32, 128), jnp.float32),
            pltpu.VMEM((256, 128), jnp.float32),
            pltpu.VMEM((8 * devices, 128), jnp.float32),
            pltpu.VMEM((8 * devices, 128), jnp.float32),
            pltpu.VMEM((grid_rows, 8, 128), jnp.float32),
            pltpu.VMEM((grid_rows, 8, 128), jnp.float32),
            pltpu.VMEM((8 * devices, 128), jnp.float32),
            pltpu.VMEM((8 * devices, 128), jnp.float32),
            pltpu.VMEM((5, 5, 8, 128), jnp.float32),
            pltpu.SemaphoreType.DMA((4,)),
            pltpu.SemaphoreType.DMA((4,)),
            pltpu.SemaphoreType.DMA,
            pltpu.SemaphoreType.DMA,
            pltpu.SemaphoreType.DMA,
            pltpu.SemaphoreType.DMA,
            pltpu.SemaphoreType.DMA,
            pltpu.SemaphoreType.DMA((6,)),
        ],
        compiler_params=pltpu.CompilerParams(
            collective_id=0, has_side_effects=True, vmem_limit_bytes=60 * 1024 * 1024
        ),
        name="lu_step",
    )(density, momentum, energy, forcing, jnp.swapaxes(coupling, 0, 1), inverse)
    state = jnp.concatenate([density[None], momentum, energy[None]], axis=0)
    return state + change


def solution(mesh):
    placed = (
        P("gx", "gy", None),
        P(None, "gx", "gy", None),
        P("gx", "gy", None),
        P(None, "gx", "gy", None),
        P(),
        P(),
    )
    nx_dev, ny_dev = mesh.shape["gx"], mesh.shape["gy"]

    def local(*args):
        if args[0].shape == (2, 16, 128) and (nx_dev, ny_dev) == (8, 4):
            return kernel_shards(nx_dev, ny_dev, *args)
        return shards(*args)

    return jax.shard_map(
        local, mesh=mesh, in_specs=placed, out_specs=P(None, "gx", "gy", None), check_vma=False
    )
```

```python
import functools

import jax
import jax.numpy as jnp
from jax import lax
from jax.experimental import pallas as pl
from jax.experimental.pallas import tpu as pltpu
from jax.sharding import PartitionSpec as P

precision_high = lax.Precision.HIGHEST
beta_coupling = 0.25
dissipation = 0.05


def extended_2(cells, sides, width):
    for axis, dim in sides:
        count = lax.axis_size(axis)
        ends = count - 1
        head = lax.slice_in_dim(cells, 0, width, axis=dim)
        tail = lax.slice_in_dim(cells, cells.shape[dim] - width, cells.shape[dim], axis=dim)
        cells = jnp.concatenate(
            [
                lax.ppermute(tail, axis, [(i, (i + 1) % count) for i in range(ends)]),
                cells,
                lax.ppermute(head, axis, [((i + 1) % count, i) for i in range(ends)]),
            ],
            axis=dim,
        )
    return cells


def from_behind(block, axis, distance):
    devices = range(lax.axis_size(axis))
    route = [(i - distance, i) for i in devices if i - distance in devices]
    return lax.ppermute(block, axis, route)


def apply_block(matrix, field):
    return jnp.einsum("ab,b...->a...", matrix, field, precision=precision_high)


def fluxes(state):
    density_safe = jnp.where(state[0] > 0.1, state[0], 1.0)
    momentum = state[1:4]
    energy = state[4]
    pressure = 0.4 * (energy - 0.5 * jnp.sum(momentum * momentum, axis=0) / density_safe)
    results = []
    for direction in range(3):
        velocity = momentum[direction] / density_safe
        components = [momentum[direction]]
        for component in range(3):
            extra = pressure if component == direction else 0.0
            components.append(momentum[component] * velocity + extra)
        components.append((energy + pressure) * velocity)
        results.append(jnp.stack(components))
    return jnp.stack(results)


def offset_core(array, axis, offset):
    lead_dims = array.ndim - 3
    slicer = [slice(None)] * lead_dims + [slice(2, -2), slice(2, -2), slice(2, -2)]
    length = array.shape[lead_dims + axis]
    slicer[lead_dims + axis] = slice(2 + offset, length - 2 + offset)
    return array[tuple(slicer)]


def residual_rhs(ext_state, ext_flux, forcing):
    residual_sum = forcing
    for direction in range(3):
        flux_dir = ext_flux[direction]
        residual_sum = residual_sum - 0.5 * (
            offset_core(flux_dir, direction, 1) - offset_core(flux_dir, direction, -1)
        )
        fourth = (
            offset_core(ext_state, direction, -2)
            - 4.0 * offset_core(ext_state, direction, -1)
            + 6.0 * offset_core(ext_state, direction, 0)
            - 4.0 * offset_core(ext_state, direction, 1)
            + offset_core(ext_state, direction, 2)
        )
        residual_sum = residual_sum - dissipation * fourth
    return residual_sum


def jacobian_term(matrix, sign_flip, velocity, field):
    return beta_coupling * (apply_block(matrix, field) + sign_flip * velocity * field)


def sweep(
    lead_term, cell_scale, vel_x, vel_y, mat_x, mat_y, sign_flip, west_face, south_face, inverse
):
    extent_x = lead_term.shape[1]
    extent_y = lead_term.shape[2]
    row_ids = jnp.arange(extent_x, dtype=jnp.int32)
    col_ids = jnp.arange(extent_y, dtype=jnp.int32)

    def step(state_carry, diag_num):
        prev_x, prev_y = state_carry
        columns = diag_num - row_ids
        is_valid = (columns >= 0) & (columns < extent_y)
        col_clip = jnp.clip(columns, 0, extent_y - 1)
        west_edge = lax.dynamic_index_in_dim(
            west_face, jnp.clip(diag_num, 0, extent_y - 1), axis=1, keepdims=True
        )
        from_west = jnp.concatenate([west_edge, prev_x[:, :-1]], axis=1)
        from_south = jnp.where((columns == 0)[None, :, None], south_face, prev_y)
        cell_lead = lead_term[:, row_ids, col_clip]
        scale_cells = cell_scale[row_ids, col_clip]
        fresh_cells = cell_lead - apply_block(inverse, from_west + from_south) / scale_cells
        fresh_cells = jnp.where(is_valid[None, :, None], fresh_cells, 0.0)
        jac_x = jacobian_term(mat_x, sign_flip, vel_x[row_ids, col_clip], fresh_cells)
        jac_y = jacobian_term(mat_y, sign_flip, vel_y[row_ids, col_clip], fresh_cells)
        return ((jac_x, jac_y), fresh_cells)

    initial = jnp.zeros((lead_term.shape[0], extent_x, lead_term.shape[3]), lead_term.dtype)
    diag_ids = jnp.arange(extent_x + extent_y - 1, dtype=jnp.int32)
    _, diagonals = lax.scan(step, (initial, initial), diag_ids)
    whole_block = diagonals[row_ids[:, None] + col_ids[None, :], :, row_ids[:, None], :]
    return jnp.transpose(whole_block, (2, 0, 1, 3))


def flip_field(array):
    return jnp.flip(array, axis=(array.ndim - 3, array.ndim - 2))


def wavefront(
    lead_term,
    cell_scale,
    vel_x,
    vel_y,
    mat_x,
    mat_y,
    sign_flip,
    inverse,
    chain_pos,
    blocks,
    send_x,
    send_y,
):
    nvars, extent_x, extent_y, extent_z = lead_term.shape
    block_depth = extent_z // blocks
    sections = blocks + lax.axis_size("gx") + lax.axis_size("gy") - 2

    def section(section_num, state_carry):
        whole_block, west_face, south_face = state_carry
        block_num = section_num - chain_pos
        is_active = (block_num >= 0) & (block_num < blocks)

        def work(current):
            solved = sweep(
                lead_term,
                cell_scale,
                vel_x,
                vel_y,
                mat_x,
                mat_y,
                sign_flip,
                west_face,
                south_face,
                inverse,
            )
            east_out = jacobian_term(mat_x, sign_flip, vel_x[-1], solved[:, -1])
            north_out = jacobian_term(mat_y, sign_flip, vel_y[:, -1], solved[:, :, -1])
            return (solved, east_out, north_out)

        def skip(current):
            return (
                current,
                jnp.zeros((nvars, extent_y, block_depth), jnp.float32),
                jnp.zeros((nvars, extent_x, block_depth), jnp.float32),
            )

        whole_block, east_out, north_out = lax.cond(is_active, work, skip, whole_block)
        return (whole_block, send_x(east_out), send_y(north_out))

    initial = (
        jnp.zeros_like(lead_term),
        jnp.zeros((nvars, extent_y, block_depth), jnp.float32),
        jnp.zeros((nvars, extent_x, block_depth), jnp.float32),
    )
    whole_block, _, _ = lax.fori_loop(0, sections, section, initial)
    return whole_block


def shards(density, momentum, energy, forcing, coupling, inverse):
    state = jnp.concatenate([density[None], momentum, energy[None]], axis=0)
    nvars = state.shape[0]
    z_pad = ((0, 0), (0, 0), (0, 0), (2, 2))
    own_flux = fluxes(state)
    stacked = jnp.concatenate([state, own_flux.reshape((3 * nvars,) + state.shape[1:])], axis=0)
    extended = extended_2(stacked, (("gx", 1), ("gy", 2)), 2)
    extended = jnp.pad(extended, z_pad)
    ext_state = extended[:nvars]
    ext_flux = extended[nvars:].reshape((3, nvars) + extended.shape[1:])
    rsd = residual_rhs(ext_state, ext_flux, forcing)
    vel_x = momentum[0] / density
    vel_y = momentum[1] / density
    vel_z = momentum[2] / density
    cell_scale = 1.0 + vel_x * vel_x + vel_y * vel_y + vel_z * vel_z
    lead_term = apply_block(inverse, rsd) / cell_scale
    blocks = 1
    pos_x = lax.axis_index("gx")
    pos_y = lax.axis_index("gy")
    lower_pos = pos_x + pos_y
    upper_pos = lax.axis_size("gx") - 1 - pos_x + (lax.axis_size("gy") - 1 - pos_y)

    def lower_send_x(face):
        return from_behind(face, "gx", 1)

    def lower_send_y(face):
        return from_behind(face, "gy", 1)

    def upper_send_x(face):
        return from_behind(face, "gx", -1)

    def upper_send_y(face):
        return from_behind(face, "gy", -1)

    lower = wavefront(
        lead_term,
        cell_scale,
        vel_x,
        vel_y,
        coupling[0],
        coupling[1],
        1.0,
        inverse,
        lower_pos,
        blocks,
        lower_send_x,
        lower_send_y,
    )
    upper = wavefront(
        flip_field(lower),
        flip_field(cell_scale),
        flip_field(vel_x),
        flip_field(vel_y),
        coupling[0].T,
        coupling[1].T,
        -1.0,
        inverse,
        upper_pos,
        blocks,
        upper_send_x,
        upper_send_y,
    )
    return state + flip_field(upper)


SKEW = 4
UNROLL = 16


def flux_of(rho, mom, energy, direction):
    safe = jnp.where(rho > 0.1, rho, 1.0)
    inv_rho = 1.0 / safe
    kinetic = mom[0] * mom[0] + mom[1] * mom[1] + mom[2] * mom[2]
    pressure = 0.4 * (energy - 0.5 * kinetic * inv_rho)
    velocity = mom[direction] * inv_rho
    parts = [mom[direction]]
    for component in range(3):
        part = mom[component] * velocity
        parts.append(part + pressure if component == direction else part)
    parts.append((energy + pressure) * velocity)
    return parts


def spread(vector, row):
    return jnp.broadcast_to(vector[row : row + 1, :], vector.shape)


def step_kernel(
    nx_dev,
    ny_dev,
    density_hbm,
    momentum_hbm,
    energy_hbm,
    forcing_hbm,
    coupling_hbm,
    inverse_hbm,
    w_ref,
    ext,
    forcing,
    coupling,
    inverse,
    flux_y,
    pack,
    out_a,
    in_a,
    grid_a,
    grid_b,
    out_b,
    in_b,
    coef,
    halo_send,
    halo_recv,
    a_send,
    a_recv,
    b_send,
    b_recv,
    own_sem,
    load_sem,
):
    devices = nx_dev * ny_dev
    gx = lax.axis_index("gx")
    gy = lax.axis_index("gy")
    me = gy * nx_dev + gx
    mesh_id = pl.DeviceIdType.MESH

    def place(slot):
        return (lax.rem(slot, nx_dev), lax.div(slot, nx_dev))

    def other(offset):
        return lax.rem(me + offset, devices)

    middle = (slice(2, 4), slice(8, 24), slice(None))
    loads = [
        pltpu.make_async_copy(source, target, load_sem.at[number])
        for number, (source, target) in enumerate(
            (
                (density_hbm, ext.at[(0,) + middle]),
                (momentum_hbm, ext.at[(slice(1, 4),) + middle]),
                (energy_hbm, ext.at[(4,) + middle]),
                (forcing_hbm, forcing),
                (coupling_hbm, coupling),
                (inverse_hbm, inverse),
            )
        )
    ]
    for load in loads:
        load.start()

    barrier = pltpu.get_barrier_semaphore()

    @pl.loop(1, devices)
    def _(offset):
        pl.semaphore_signal(barrier, inc=1, device_id=place(other(offset)), device_id_type=mesh_id)

    @pl.when(gx == 0)
    def _():
        ext[:, 0:2, 8:24, :] = jnp.zeros((5, 2, 16, 128), jnp.float32)

    @pl.when(gx == nx_dev - 1)
    def _():
        ext[:, 4:6, 8:24, :] = jnp.zeros((5, 2, 16, 128), jnp.float32)

    @pl.when(gy == 0)
    def _():
        ext[:, 2:4, 0:8, :] = jnp.zeros((5, 2, 8, 128), jnp.float32)

    @pl.when(gy == ny_dev - 1)
    def _():
        ext[:, 2:4, 24:32, :] = jnp.zeros((5, 2, 8, 128), jnp.float32)

    loads[4].wait()
    loads[5].wait()
    row_id = lax.broadcasted_iota(jnp.int32, (8, 128), 0)
    inv_cols = []
    for c in range(5):
        column = jnp.zeros((8, 128), jnp.float32)
        for a in range(5):
            column = jnp.where(row_id == a, 0.25 * inverse[a, c], column)
        inv_cols.append(column)
        coef[4, c] = column
    for d in range(2):
        for b in range(5):
            lower = inv_cols[0] * coupling[0, d, b]
            upper = inv_cols[0] * coupling[b, d, 0]
            for c in range(1, 5):
                lower = lower + inv_cols[c] * coupling[c, d, b]
                upper = upper + inv_cols[c] * coupling[b, d, c]
            coef[d, b] = lower
            coef[2 + d, b] = upper
    grid_a[...] = jnp.zeros(grid_a.shape, jnp.float32)
    grid_b[...] = jnp.zeros(grid_b.shape, jnp.float32)

    for load in loads[:3]:
        load.wait()
    pl.semaphore_wait(barrier, devices - 1)

    block = ext.at[:, 2:4, 8:24, :]
    to_east = pltpu.make_async_remote_copy(
        block, ext.at[:, 0:2, 8:24, :], halo_send.at[0], halo_recv.at[0], (gx + 1, gy), mesh_id
    )
    to_west = pltpu.make_async_remote_copy(
        block, ext.at[:, 4:6, 8:24, :], halo_send.at[1], halo_recv.at[1], (gx - 1, gy), mesh_id
    )
    to_north = pltpu.make_async_remote_copy(
        ext.at[:, 2:4, 16:24, :],
        ext.at[:, 2:4, 0:8, :],
        halo_send.at[2],
        halo_recv.at[2],
        (gx, gy + 1),
        mesh_id,
    )
    to_south = pltpu.make_async_remote_copy(
        ext.at[:, 2:4, 8:16, :],
        ext.at[:, 2:4, 24:32, :],
        halo_send.at[3],
        halo_recv.at[3],
        (gx, gy - 1),
        mesh_id,
    )
    sides = (
        (to_east, gx < nx_dev - 1, gx > 0),
        (to_west, gx > 0, gx < nx_dev - 1),
        (to_north, gy < ny_dev - 1, gy > 0),
        (to_south, gy > 0, gy < ny_dev - 1),
    )
    for copy, sends, _ in sides:
        pl.when(sends)(copy.start)

    loads[3].wait()
    rho, *mom, en = [ext[f, 2:4, 8:24, :] for f in range(5)]
    inv_rho = 1.0 / rho
    vel = [m * inv_rho for m in mom]
    inv_scale = 1.0 / (1.0 + vel[0] * vel[0] + vel[1] * vel[1] + vel[2] * vel[2])
    own = [rho] + mom + [en]
    flux_z = flux_of(rho, mom, en, 2)
    lane3 = lax.broadcasted_iota(jnp.int32, (2, 16, 128), 2)

    def from_z(field, offset):
        moved = pltpu.roll(field.reshape(32, 128), (-offset) % 128, 1).reshape(2, 16, 128)
        inside = (lane3 < 128 - offset) if offset > 0 else (lane3 >= -offset)
        return jnp.where(inside, moved, 0.0)

    rsd = []
    for f in range(5):
        total = forcing[f] - (18.0 * dissipation) * own[f]
        total = total + from_z(4.0 * dissipation * own[f] - 0.5 * flux_z[f], 1)
        total = total + from_z(4.0 * dissipation * own[f] + 0.5 * flux_z[f], -1)
        total = total - dissipation * (from_z(own[f], 2) + from_z(own[f], -2))
        rsd.append(total)

    for copy, _, receives in sides:
        pl.when(receives)(copy.wait_recv)

    wide = [ext[f, 1:5, 8:24, :] for f in range(5)]
    flux_x = flux_of(wide[0], wide[1:4], wide[4], 0)
    tall = [ext[f, 2:4, :, :] for f in range(5)]
    for f, part in enumerate(flux_of(tall[0], tall[1:4], tall[4], 1)):
        flux_y[f] = part
    for f in range(5):
        total = rsd[f] - 0.5 * (flux_x[f][2:4] - flux_x[f][0:2])
        total = total - 0.5 * (flux_y[f, :, 9:25, :] - flux_y[f, :, 7:23, :])
        near = (wide[f][0:2] + wide[f][2:4]) + (ext[f, 2:4, 7:23, :] + ext[f, 2:4, 9:25, :])
        far = (ext[f, 0:2, 8:24, :] + ext[f, 4:6, 8:24, :]) + (
            ext[f, 2:4, 6:22, :] + ext[f, 2:4, 10:26, :]
        )
        rsd[f] = total + dissipation * (4.0 * near - far)

    fields = []
    for a in range(5):
        total = inverse[a, 0] * rsd[0]
        for b in range(1, 5):
            total = total + inverse[a, b] * rsd[b]
        fields.append(total * inv_scale)
    fields += [vel[0], vel[1], inv_scale]

    for xl in range(2):
        for f in range(8):
            pack[pl.ds(xl * 128 + f, 16, stride=8), :] = fields[f][xl]
        turned = pack[xl * 128 : (xl + 1) * 128, :].T
        for part in range(4):
            out_a[pl.ds(xl * 4 + part, 32, stride=8), :] = turned[part * 32 : (part + 1) * 32]

    def tile(ref, slot):
        return ref.at[pl.ds(pl.multiple_of(slot * 8, 8), 8), :]

    def exchange(source, target, send, recv):
        @pl.loop(1, devices)
        def _(offset):
            slot = other(offset)
            pltpu.make_async_remote_copy(
                tile(source, slot), tile(target, me), send, recv, place(slot), mesh_id
            ).start()

        mine = pltpu.make_async_copy(tile(source, me), tile(target, me), own_sem)
        mine.start()
        mine.wait()
        rows = pl.ds(0, 8 * (devices - 1))
        whole = pltpu.make_async_remote_copy(
            source.at[rows, :], target.at[rows, :], send, recv, place(other(1)), mesh_id
        )
        whole.wait_recv()
        return whole.wait_send

    finish_a = exchange(out_a, in_a, a_send, a_recv)

    lane = lax.broadcasted_iota(jnp.int32, (128, 128), 1)
    low = lane < 64
    front = 8 * SKEW
    for pair in range(ny_dev // 2):
        turned = in_a[pair * 128 : (pair + 1) * 128, :].T
        first = front + pair * 32
        grid_a[first : first + 16] = jnp.where(low, turned, 0.0).reshape(16, 8, 128)
        turned = pltpu.roll(turned, 64, 1)
        grid_a[first + 16 : first + 32] = jnp.where(low, turned, 0.0).reshape(16, 8, 128)

    extent_y = 16 * ny_dev
    lane_x = lax.broadcasted_iota(jnp.int32, (1, 8, 128), 2) // 4
    buffers = (grid_a, grid_b)
    for bit in range(4):
        source, target = buffers[bit % 2], buffers[1 - bit % 2]
        shift = SKEW << bit
        rows = extent_y + SKEW * ((2 << bit) - 1)
        odd = (lane_x // (1 << bit)) % 2 == 1
        target[front : front + rows] = jnp.where(
            odd, source[front - shift : front - shift + rows], source[front : front + rows]
        )

    steps = extent_y + 15 * SKEW
    steps = -(-steps // UNROLL) * UNROLL
    zero = jnp.zeros((8, 128), jnp.float32)

    def run_sweep(first_coef, sign, roll_by, row_of):
        mat_x = [coef[first_coef, b] for b in range(5)]
        mat_y = [coef[first_coef + 1, b] for b in range(5)]
        mat_i = [coef[4, b] for b in range(5)]

        def advance(index, carry):
            first, second, third, *queue = carry
            for inner in range(UNROLL):
                row = row_of(index * UNROLL + inner)
                after = spread(grid_a[row_of(index * UNROLL + inner + 1)], 7)
                cells = grid_a[row]
                speed_x = sign * spread(cells, 5)
                speed_y = sign * spread(cells, 6)
                cells = cells - spread(cells, 7) * pltpu.roll(queue.pop(0), roll_by, 1)
                cells = ((cells - first) - second) - third
                grid_a[row] = cells
                values = [spread(cells, b) for b in range(5)]
                terms = [((mat_y[b] + speed_y * mat_i[b]) * after) * values[b] for b in range(5)]
                first, second, third = terms[0], terms[1] + terms[2], terms[3] + terms[4]
                terms = [(mat_x[b] + speed_x * mat_i[b]) * values[b] for b in range(5)]
                queue.append(((terms[0] + terms[1]) + (terms[2] + terms[3])) + terms[4])
            return (first, second, third, *queue)

        lax.fori_loop(0, steps // UNROLL, advance, (zero,) * (3 + SKEW))

    run_sweep(0, 1.0, 4, lambda step: front + step)
    run_sweep(2, -1.0, 124, lambda step: front + steps - 1 - step)

    for turn, bit in enumerate((3, 2, 1, 0)):
        source, target = buffers[turn % 2], buffers[1 - turn % 2]
        shift = SKEW << bit
        rows = extent_y + SKEW * ((1 << bit) - 1)
        odd = (lane_x // (1 << bit)) % 2 == 1
        target[front : front + rows] = jnp.where(
            odd, source[front + shift : front + shift + rows], source[front : front + rows]
        )

    for pair in range(ny_dev // 2):
        first = front + pair * 32
        left = grid_a[first : first + 16].reshape(128, 128)
        right = pltpu.roll(grid_a[first + 16 : first + 32].reshape(128, 128), 64, 1)
        out_b[pair * 128 : (pair + 1) * 128, :] = jnp.where(low, left, right).T

    finish_b = exchange(out_b, in_b, b_send, b_recv)

    for xl in range(2):
        planes = [in_b[pl.ds(xl * 4 + part, 32, stride=8), :] for part in range(4)]
        pack[xl * 128 : (xl + 1) * 128, :] = jnp.concatenate(planes, axis=0).T
        for f in range(5):
            w_ref[f, xl] = pack[pl.ds(xl * 128 + f, 16, stride=8), :]

    for copy, sends, _ in sides:
        pl.when(sends)(copy.wait_send)
    finish_a()
    finish_b()


def kernel_shards(nx_dev, ny_dev, density, momentum, energy, forcing, coupling, inverse):
    devices = nx_dev * ny_dev
    grid_rows = 8 * SKEW + 16 * ny_dev + 15 * SKEW + UNROLL
    vmem = pl.BlockSpec(memory_space=pltpu.VMEM)
    change = pl.pallas_call(
        functools.partial(step_kernel, nx_dev, ny_dev),
        out_shape=jax.ShapeDtypeStruct((5, 2, 16, 128), jnp.float32),
        in_specs=[pl.BlockSpec(memory_space=pltpu.HBM)] * 6,
        out_specs=vmem,
        scratch_shapes=[
            pltpu.VMEM((5, 6, 32, 128), jnp.float32),
            pltpu.VMEM((5, 2, 16, 128), jnp.float32),
            pltpu.SMEM((5, 2, 5), jnp.float32),
            pltpu.SMEM((5, 5), jnp.float32),
            pltpu.VMEM((5, 2, 32, 128), jnp.float32),
            pltpu.VMEM((256, 128), jnp.float32),
            pltpu.VMEM((8 * devices, 128), jnp.float32),
            pltpu.VMEM((8 * devices, 128), jnp.float32),
            pltpu.VMEM((grid_rows, 8, 128), jnp.float32),
            pltpu.VMEM((grid_rows, 8, 128), jnp.float32),
            pltpu.VMEM((8 * devices, 128), jnp.float32),
            pltpu.VMEM((8 * devices, 128), jnp.float32),
            pltpu.VMEM((5, 5, 8, 128), jnp.float32),
            pltpu.SemaphoreType.DMA((4,)),
            pltpu.SemaphoreType.DMA((4,)),
            pltpu.SemaphoreType.DMA,
            pltpu.SemaphoreType.DMA,
            pltpu.SemaphoreType.DMA,
            pltpu.SemaphoreType.DMA,
            pltpu.SemaphoreType.DMA,
            pltpu.SemaphoreType.DMA((6,)),
        ],
        compiler_params=pltpu.CompilerParams(
            collective_id=0, has_side_effects=True, vmem_limit_bytes=60 * 1024 * 1024
        ),
        name="lu_step",
    )(density, momentum, energy, forcing, jnp.swapaxes(coupling, 0, 1), inverse)
    state = jnp.concatenate([density[None], momentum, energy[None]], axis=0)
    return state + change


def solution(mesh):
    placed = (
        P("gx", "gy", None),
        P(None, "gx", "gy", None),
        P("gx", "gy", None),
        P(None, "gx", "gy", None),
        P(),
        P(),
    )
    nx_dev, ny_dev = mesh.shape["gx"], mesh.shape["gy"]

    def local(*args):
        if args[0].shape == (2, 16, 128) and (nx_dev, ny_dev) == (8, 4):
            return kernel_shards(nx_dev, ny_dev, *args)
        return shards(*args)

    return jax.shard_map(
        local, mesh=mesh, in_specs=placed, out_specs=P(None, "gx", "gy", None), check_vma=False
    )
```

```python
import functools

import jax
import jax.numpy as jnp
from jax import lax
from jax.experimental import pallas as pl
from jax.experimental.pallas import tpu as pltpu
from jax.sharding import PartitionSpec as P

precision_high = lax.Precision.HIGHEST
beta_coupling = 0.25
dissipation = 0.05


def extended_2(cells, sides, width):
    for axis, dim in sides:
        count = lax.axis_size(axis)
        ends = count - 1
        head = lax.slice_in_dim(cells, 0, width, axis=dim)
        tail = lax.slice_in_dim(cells, cells.shape[dim] - width, cells.shape[dim], axis=dim)
        cells = jnp.concatenate(
            [
                lax.ppermute(tail, axis, [(i, (i + 1) % count) for i in range(ends)]),
                cells,
                lax.ppermute(head, axis, [((i + 1) % count, i) for i in range(ends)]),
            ],
            axis=dim,
        )
    return cells


def from_behind(block, axis, distance):
    devices = range(lax.axis_size(axis))
    route = [(i - distance, i) for i in devices if i - distance in devices]
    return lax.ppermute(block, axis, route)


def apply_block(matrix, field):
    return jnp.einsum("ab,b...->a...", matrix, field, precision=precision_high)


def fluxes(state):
    density_safe = jnp.where(state[0] > 0.1, state[0], 1.0)
    momentum = state[1:4]
    energy = state[4]
    pressure = 0.4 * (energy - 0.5 * jnp.sum(momentum * momentum, axis=0) / density_safe)
    results = []
    for direction in range(3):
        velocity = momentum[direction] / density_safe
        components = [momentum[direction]]
        for component in range(3):
            extra = pressure if component == direction else 0.0
            components.append(momentum[component] * velocity + extra)
        components.append((energy + pressure) * velocity)
        results.append(jnp.stack(components))
    return jnp.stack(results)


def offset_core(array, axis, offset):
    lead_dims = array.ndim - 3
    slicer = [slice(None)] * lead_dims + [slice(2, -2), slice(2, -2), slice(2, -2)]
    length = array.shape[lead_dims + axis]
    slicer[lead_dims + axis] = slice(2 + offset, length - 2 + offset)
    return array[tuple(slicer)]


def residual_rhs(ext_state, ext_flux, forcing):
    residual_sum = forcing
    for direction in range(3):
        flux_dir = ext_flux[direction]
        residual_sum = residual_sum - 0.5 * (
            offset_core(flux_dir, direction, 1) - offset_core(flux_dir, direction, -1)
        )
        fourth = (
            offset_core(ext_state, direction, -2)
            - 4.0 * offset_core(ext_state, direction, -1)
            + 6.0 * offset_core(ext_state, direction, 0)
            - 4.0 * offset_core(ext_state, direction, 1)
            + offset_core(ext_state, direction, 2)
        )
        residual_sum = residual_sum - dissipation * fourth
    return residual_sum


def jacobian_term(matrix, sign_flip, velocity, field):
    return beta_coupling * (apply_block(matrix, field) + sign_flip * velocity * field)


def sweep(
    lead_term, cell_scale, vel_x, vel_y, mat_x, mat_y, sign_flip, west_face, south_face, inverse
):
    extent_x = lead_term.shape[1]
    extent_y = lead_term.shape[2]
    row_ids = jnp.arange(extent_x, dtype=jnp.int32)
    col_ids = jnp.arange(extent_y, dtype=jnp.int32)

    def step(state_carry, diag_num):
        prev_x, prev_y = state_carry
        columns = diag_num - row_ids
        is_valid = (columns >= 0) & (columns < extent_y)
        col_clip = jnp.clip(columns, 0, extent_y - 1)
        west_edge = lax.dynamic_index_in_dim(
            west_face, jnp.clip(diag_num, 0, extent_y - 1), axis=1, keepdims=True
        )
        from_west = jnp.concatenate([west_edge, prev_x[:, :-1]], axis=1)
        from_south = jnp.where((columns == 0)[None, :, None], south_face, prev_y)
        cell_lead = lead_term[:, row_ids, col_clip]
        scale_cells = cell_scale[row_ids, col_clip]
        fresh_cells = cell_lead - apply_block(inverse, from_west + from_south) / scale_cells
        fresh_cells = jnp.where(is_valid[None, :, None], fresh_cells, 0.0)
        jac_x = jacobian_term(mat_x, sign_flip, vel_x[row_ids, col_clip], fresh_cells)
        jac_y = jacobian_term(mat_y, sign_flip, vel_y[row_ids, col_clip], fresh_cells)
        return ((jac_x, jac_y), fresh_cells)

    initial = jnp.zeros((lead_term.shape[0], extent_x, lead_term.shape[3]), lead_term.dtype)
    diag_ids = jnp.arange(extent_x + extent_y - 1, dtype=jnp.int32)
    _, diagonals = lax.scan(step, (initial, initial), diag_ids)
    whole_block = diagonals[row_ids[:, None] + col_ids[None, :], :, row_ids[:, None], :]
    return jnp.transpose(whole_block, (2, 0, 1, 3))


def flip_field(array):
    return jnp.flip(array, axis=(array.ndim - 3, array.ndim - 2))


def wavefront(
    lead_term,
    cell_scale,
    vel_x,
    vel_y,
    mat_x,
    mat_y,
    sign_flip,
    inverse,
    chain_pos,
    blocks,
    send_x,
    send_y,
):
    nvars, extent_x, extent_y, extent_z = lead_term.shape
    block_depth = extent_z // blocks
    sections = blocks + lax.axis_size("gx") + lax.axis_size("gy") - 2

    def section(section_num, state_carry):
        whole_block, west_face, south_face = state_carry
        block_num = section_num - chain_pos
        is_active = (block_num >= 0) & (block_num < blocks)

        def work(current):
            solved = sweep(
                lead_term,
                cell_scale,
                vel_x,
                vel_y,
                mat_x,
                mat_y,
                sign_flip,
                west_face,
                south_face,
                inverse,
            )
            east_out = jacobian_term(mat_x, sign_flip, vel_x[-1], solved[:, -1])
            north_out = jacobian_term(mat_y, sign_flip, vel_y[:, -1], solved[:, :, -1])
            return (solved, east_out, north_out)

        def skip(current):
            return (
                current,
                jnp.zeros((nvars, extent_y, block_depth), jnp.float32),
                jnp.zeros((nvars, extent_x, block_depth), jnp.float32),
            )

        whole_block, east_out, north_out = lax.cond(is_active, work, skip, whole_block)
        return (whole_block, send_x(east_out), send_y(north_out))

    initial = (
        jnp.zeros_like(lead_term),
        jnp.zeros((nvars, extent_y, block_depth), jnp.float32),
        jnp.zeros((nvars, extent_x, block_depth), jnp.float32),
    )
    whole_block, _, _ = lax.fori_loop(0, sections, section, initial)
    return whole_block


def shards(density, momentum, energy, forcing, coupling, inverse):
    state = jnp.concatenate([density[None], momentum, energy[None]], axis=0)
    nvars = state.shape[0]
    z_pad = ((0, 0), (0, 0), (0, 0), (2, 2))
    own_flux = fluxes(state)
    stacked = jnp.concatenate([state, own_flux.reshape((3 * nvars,) + state.shape[1:])], axis=0)
    extended = extended_2(stacked, (("gx", 1), ("gy", 2)), 2)
    extended = jnp.pad(extended, z_pad)
    ext_state = extended[:nvars]
    ext_flux = extended[nvars:].reshape((3, nvars) + extended.shape[1:])
    rsd = residual_rhs(ext_state, ext_flux, forcing)
    vel_x = momentum[0] / density
    vel_y = momentum[1] / density
    vel_z = momentum[2] / density
    cell_scale = 1.0 + vel_x * vel_x + vel_y * vel_y + vel_z * vel_z
    lead_term = apply_block(inverse, rsd) / cell_scale
    blocks = 1
    pos_x = lax.axis_index("gx")
    pos_y = lax.axis_index("gy")
    lower_pos = pos_x + pos_y
    upper_pos = lax.axis_size("gx") - 1 - pos_x + (lax.axis_size("gy") - 1 - pos_y)

    def lower_send_x(face):
        return from_behind(face, "gx", 1)

    def lower_send_y(face):
        return from_behind(face, "gy", 1)

    def upper_send_x(face):
        return from_behind(face, "gx", -1)

    def upper_send_y(face):
        return from_behind(face, "gy", -1)

    lower = wavefront(
        lead_term,
        cell_scale,
        vel_x,
        vel_y,
        coupling[0],
        coupling[1],
        1.0,
        inverse,
        lower_pos,
        blocks,
        lower_send_x,
        lower_send_y,
    )
    upper = wavefront(
        flip_field(lower),
        flip_field(cell_scale),
        flip_field(vel_x),
        flip_field(vel_y),
        coupling[0].T,
        coupling[1].T,
        -1.0,
        inverse,
        upper_pos,
        blocks,
        upper_send_x,
        upper_send_y,
    )
    return state + flip_field(upper)


SKEW = 4
UNROLL = 16


def flux_of(rho, mom, energy, direction):
    safe = jnp.where(rho > 0.1, rho, 1.0)
    inv_rho = 1.0 / safe
    kinetic = mom[0] * mom[0] + mom[1] * mom[1] + mom[2] * mom[2]
    pressure = 0.4 * (energy - 0.5 * kinetic * inv_rho)
    velocity = mom[direction] * inv_rho
    parts = [mom[direction]]
    for component in range(3):
        part = mom[component] * velocity
        parts.append(part + pressure if component == direction else part)
    parts.append((energy + pressure) * velocity)
    return parts


def spread(vector, row):
    return jnp.broadcast_to(vector[row : row + 1, :], vector.shape)


def step_kernel(
    nx_dev,
    ny_dev,
    density_hbm,
    momentum_hbm,
    energy_hbm,
    forcing_hbm,
    coupling_hbm,
    inverse_hbm,
    w_ref,
    ext,
    forcing,
    coupling,
    inverse,
    flux_y,
    pack,
    out_a,
    in_a,
    grid_a,
    grid_b,
    out_b,
    in_b,
    coef,
    halo_send,
    halo_recv,
    a_send,
    a_recv,
    b_send,
    b_recv,
    own_sem,
    load_sem,
):
    devices = nx_dev * ny_dev
    gx = lax.axis_index("gx")
    gy = lax.axis_index("gy")
    me = gy * nx_dev + gx
    mesh_id = pl.DeviceIdType.MESH

    def place(slot):
        return (lax.rem(slot, nx_dev), lax.div(slot, nx_dev))

    def other(offset):
        return lax.rem(me + offset, devices)

    barrier = pltpu.get_barrier_semaphore()

    @pl.loop(1, devices)
    def _(offset):
        pl.semaphore_signal(barrier, inc=1, device_id=place(other(offset)), device_id_type=mesh_id)

    middle = (slice(2, 4), slice(8, 24), slice(None))
    loads = [
        pltpu.make_async_copy(source, target, load_sem.at[number])
        for number, (source, target) in enumerate(
            (
                (density_hbm, ext.at[(0,) + middle]),
                (momentum_hbm, ext.at[(slice(1, 4),) + middle]),
                (energy_hbm, ext.at[(4,) + middle]),
                (forcing_hbm, forcing),
                (coupling_hbm, coupling),
                (inverse_hbm, inverse),
            )
        )
    ]
    for load in loads:
        load.start()

    @pl.when(gx == 0)
    def _():
        ext[:, 0:2, 8:24, :] = jnp.zeros((5, 2, 16, 128), jnp.float32)

    @pl.when(gx == nx_dev - 1)
    def _():
        ext[:, 4:6, 8:24, :] = jnp.zeros((5, 2, 16, 128), jnp.float32)

    @pl.when(gy == 0)
    def _():
        ext[:, 2:4, 0:8, :] = jnp.zeros((5, 2, 8, 128), jnp.float32)

    @pl.when(gy == ny_dev - 1)
    def _():
        ext[:, 2:4, 24:32, :] = jnp.zeros((5, 2, 8, 128), jnp.float32)

    loads[4].wait()
    loads[5].wait()
    row_id = lax.broadcasted_iota(jnp.int32, (8, 128), 0)
    inv_cols = []
    for c in range(5):
        column = jnp.zeros((8, 128), jnp.float32)
        for a in range(5):
            column = jnp.where(row_id == a, 0.25 * inverse[a, c], column)
        inv_cols.append(column)
        coef[4, c] = column
    for d in range(2):
        for b in range(5):
            lower = inv_cols[0] * coupling[0, d, b]
            upper = inv_cols[0] * coupling[b, d, 0]
            for c in range(1, 5):
                lower = lower + inv_cols[c] * coupling[c, d, b]
                upper = upper + inv_cols[c] * coupling[b, d, c]
            coef[d, b] = lower
            coef[2 + d, b] = upper
    grid_a[...] = jnp.zeros(grid_a.shape, jnp.float32)
    grid_b[...] = jnp.zeros(grid_b.shape, jnp.float32)

    for load in loads[:3]:
        load.wait()
    pl.semaphore_wait(barrier, devices - 1)

    block = ext.at[:, 2:4, 8:24, :]
    to_east = pltpu.make_async_remote_copy(
        block, ext.at[:, 0:2, 8:24, :], halo_send.at[0], halo_recv.at[0], (gx + 1, gy), mesh_id
    )
    to_west = pltpu.make_async_remote_copy(
        block, ext.at[:, 4:6, 8:24, :], halo_send.at[1], halo_recv.at[1], (gx - 1, gy), mesh_id
    )
    to_north = pltpu.make_async_remote_copy(
        ext.at[:, 2:4, 16:24, :],
        ext.at[:, 2:4, 0:8, :],
        halo_send.at[2],
        halo_recv.at[2],
        (gx, gy + 1),
        mesh_id,
    )
    to_south = pltpu.make_async_remote_copy(
        ext.at[:, 2:4, 8:16, :],
        ext.at[:, 2:4, 24:32, :],
        halo_send.at[3],
        halo_recv.at[3],
        (gx, gy - 1),
        mesh_id,
    )
    sides = (
        (to_east, gx < nx_dev - 1, gx > 0),
        (to_west, gx > 0, gx < nx_dev - 1),
        (to_north, gy < ny_dev - 1, gy > 0),
        (to_south, gy > 0, gy < ny_dev - 1),
    )
    for copy, sends, _ in sides:
        pl.when(sends)(copy.start)

    loads[3].wait()
    rho, *mom, en = [ext[f, 2:4, 8:24, :] for f in range(5)]
    inv_rho = 1.0 / rho
    vel = [m * inv_rho for m in mom]
    inv_scale = 1.0 / (1.0 + vel[0] * vel[0] + vel[1] * vel[1] + vel[2] * vel[2])
    own = [rho] + mom + [en]
    flux_z = flux_of(rho, mom, en, 2)
    lane3 = lax.broadcasted_iota(jnp.int32, (2, 16, 128), 2)

    def from_z(field, offset):
        moved = pltpu.roll(field.reshape(32, 128), (-offset) % 128, 1).reshape(2, 16, 128)
        inside = (lane3 < 128 - offset) if offset > 0 else (lane3 >= -offset)
        return jnp.where(inside, moved, 0.0)

    rsd = []
    for f in range(5):
        total = forcing[f] - (18.0 * dissipation) * own[f]
        total = total + from_z(4.0 * dissipation * own[f] - 0.5 * flux_z[f], 1)
        total = total + from_z(4.0 * dissipation * own[f] + 0.5 * flux_z[f], -1)
        total = total - dissipation * (from_z(own[f], 2) + from_z(own[f], -2))
        rsd.append(total)

    for copy, _, receives in sides:
        pl.when(receives)(copy.wait_recv)

    wide = [ext[f, 1:5, 8:24, :] for f in range(5)]
    flux_x = flux_of(wide[0], wide[1:4], wide[4], 0)
    tall = [ext[f, 2:4, :, :] for f in range(5)]
    for f, part in enumerate(flux_of(tall[0], tall[1:4], tall[4], 1)):
        flux_y[f] = part
    for f in range(5):
        total = rsd[f] - 0.5 * (flux_x[f][2:4] - flux_x[f][0:2])
        total = total - 0.5 * (flux_y[f, :, 9:25, :] - flux_y[f, :, 7:23, :])
        near = (wide[f][0:2] + wide[f][2:4]) + (ext[f, 2:4, 7:23, :] + ext[f, 2:4, 9:25, :])
        far = (ext[f, 0:2, 8:24, :] + ext[f, 4:6, 8:24, :]) + (
            ext[f, 2:4, 6:22, :] + ext[f, 2:4, 10:26, :]
        )
        rsd[f] = total + dissipation * (4.0 * near - far)

    fields = []
    for a in range(5):
        total = inverse[a, 0] * rsd[0]
        for b in range(1, 5):
            total = total + inverse[a, b] * rsd[b]
        fields.append(total * inv_scale)
    fields += [vel[0], vel[1], inv_scale]

    for xl in range(2):
        for f in range(8):
            pack[pl.ds(xl * 128 + f, 16, stride=8), :] = fields[f][xl]
        turned = pack[xl * 128 : (xl + 1) * 128, :].T
        for part in range(4):
            out_a[pl.ds(xl * 4 + part, 32, stride=8), :] = turned[part * 32 : (part + 1) * 32]

    def tile(ref, slot):
        return ref.at[pl.ds(pl.multiple_of(slot * 8, 8), 8), :]

    def exchange(source, target, send, recv):
        @pl.loop(1, devices)
        def _(offset):
            slot = other(offset)
            pltpu.make_async_remote_copy(
                tile(source, slot), tile(target, me), send, recv, place(slot), mesh_id
            ).start()

        mine = pltpu.make_async_copy(tile(source, me), tile(target, me), own_sem)
        mine.start()
        mine.wait()
        rows = pl.ds(0, 8 * (devices - 1))
        whole = pltpu.make_async_remote_copy(
            source.at[rows, :], target.at[rows, :], send, recv, place(other(1)), mesh_id
        )
        whole.wait_recv()
        return whole.wait_send

    finish_a = exchange(out_a, in_a, a_send, a_recv)

    lane = lax.broadcasted_iota(jnp.int32, (128, 128), 1)
    low = lane < 64
    front = 8 * SKEW
    for pair in range(ny_dev // 2):
        turned = in_a[pair * 128 : (pair + 1) * 128, :].T
        first = front + pair * 32
        grid_a[first : first + 16] = jnp.where(low, turned, 0.0).reshape(16, 8, 128)
        turned = pltpu.roll(turned, 64, 1)
        grid_a[first + 16 : first + 32] = jnp.where(low, turned, 0.0).reshape(16, 8, 128)

    extent_y = 16 * ny_dev
    lane_x = lax.broadcasted_iota(jnp.int32, (1, 8, 128), 2) // 4
    buffers = (grid_a, grid_b)
    for bit in range(4):
        source, target = buffers[bit % 2], buffers[1 - bit % 2]
        shift = SKEW << bit
        rows = extent_y + SKEW * ((2 << bit) - 1)
        odd = (lane_x // (1 << bit)) % 2 == 1
        target[front : front + rows] = jnp.where(
            odd, source[front - shift : front - shift + rows], source[front : front + rows]
        )

    steps = extent_y + 15 * SKEW
    steps = -(-steps // UNROLL) * UNROLL
    zero = jnp.zeros((8, 128), jnp.float32)

    def run_sweep(first_coef, sign, roll_by, row_of):
        mat_x = [coef[first_coef, b] for b in range(5)]
        mat_y = [coef[first_coef + 1, b] for b in range(5)]
        mat_i = [coef[4, b] for b in range(5)]

        def advance(index, carry):
            first, second, third, *queue = carry
            for inner in range(UNROLL):
                row = row_of(index * UNROLL + inner)
                after = spread(grid_a[row_of(index * UNROLL + inner + 1)], 7)
                cells = grid_a[row]
                speed_x = sign * spread(cells, 5)
                speed_y = sign * spread(cells, 6)
                cells = cells - spread(cells, 7) * pltpu.roll(queue.pop(0), roll_by, 1)
                cells = ((cells - first) - second) - third
                grid_a[row] = cells
                values = [spread(cells, b) for b in range(5)]
                terms = [((mat_y[b] + speed_y * mat_i[b]) * after) * values[b] for b in range(5)]
                first, second, third = terms[0], terms[1] + terms[2], terms[3] + terms[4]
                terms = [(mat_x[b] + speed_x * mat_i[b]) * values[b] for b in range(5)]
                queue.append(((terms[0] + terms[1]) + (terms[2] + terms[3])) + terms[4])
            return (first, second, third, *queue)

        lax.fori_loop(0, steps // UNROLL, advance, (zero,) * (3 + SKEW))

    run_sweep(0, 1.0, 4, lambda step: front + step)
    run_sweep(2, -1.0, 124, lambda step: front + steps - 1 - step)

    for turn, bit in enumerate((3, 2, 1, 0)):
        source, target = buffers[turn % 2], buffers[1 - turn % 2]
        shift = SKEW << bit
        rows = extent_y + SKEW * ((1 << bit) - 1)
        odd = (lane_x // (1 << bit)) % 2 == 1
        target[front : front + rows] = jnp.where(
            odd, source[front + shift : front + shift + rows], source[front : front + rows]
        )

    for pair in range(ny_dev // 2):
        first = front + pair * 32
        left = grid_a[first : first + 16].reshape(128, 128)
        right = pltpu.roll(grid_a[first + 16 : first + 32].reshape(128, 128), 64, 1)
        out_b[pair * 128 : (pair + 1) * 128, :] = jnp.where(low, left, right).T

    finish_b = exchange(out_b, in_b, b_send, b_recv)

    for xl in range(2):
        planes = [in_b[pl.ds(xl * 4 + part, 32, stride=8), :] for part in range(4)]
        pack[xl * 128 : (xl + 1) * 128, :] = jnp.concatenate(planes, axis=0).T
        for f in range(5):
            w_ref[f, xl] = pack[pl.ds(xl * 128 + f, 16, stride=8), :]

    for copy, sends, _ in sides:
        pl.when(sends)(copy.wait_send)
    finish_a()
    finish_b()


def kernel_shards(nx_dev, ny_dev, density, momentum, energy, forcing, coupling, inverse):
    devices = nx_dev * ny_dev
    grid_rows = 8 * SKEW + 16 * ny_dev + 15 * SKEW + UNROLL
    vmem = pl.BlockSpec(memory_space=pltpu.VMEM)
    change = pl.pallas_call(
        functools.partial(step_kernel, nx_dev, ny_dev),
        out_shape=jax.ShapeDtypeStruct((5, 2, 16, 128), jnp.float32),
        in_specs=[pl.BlockSpec(memory_space=pltpu.HBM)] * 6,
        out_specs=vmem,
        scratch_shapes=[
            pltpu.VMEM((5, 6, 32, 128), jnp.float32),
            pltpu.VMEM((5, 2, 16, 128), jnp.float32),
            pltpu.SMEM((5, 2, 5), jnp.float32),
            pltpu.SMEM((5, 5), jnp.float32),
            pltpu.VMEM((5, 2, 32, 128), jnp.float32),
            pltpu.VMEM((256, 128), jnp.float32),
            pltpu.VMEM((8 * devices, 128), jnp.float32),
            pltpu.VMEM((8 * devices, 128), jnp.float32),
            pltpu.VMEM((grid_rows, 8, 128), jnp.float32),
            pltpu.VMEM((grid_rows, 8, 128), jnp.float32),
            pltpu.VMEM((8 * devices, 128), jnp.float32),
            pltpu.VMEM((8 * devices, 128), jnp.float32),
            pltpu.VMEM((5, 5, 8, 128), jnp.float32),
            pltpu.SemaphoreType.DMA((4,)),
            pltpu.SemaphoreType.DMA((4,)),
            pltpu.SemaphoreType.DMA,
            pltpu.SemaphoreType.DMA,
            pltpu.SemaphoreType.DMA,
            pltpu.SemaphoreType.DMA,
            pltpu.SemaphoreType.DMA,
            pltpu.SemaphoreType.DMA((6,)),
        ],
        compiler_params=pltpu.CompilerParams(
            collective_id=0, has_side_effects=True, vmem_limit_bytes=60 * 1024 * 1024
        ),
        name="lu_step",
    )(density, momentum, energy, forcing, jnp.swapaxes(coupling, 0, 1), inverse)
    state = jnp.concatenate([density[None], momentum, energy[None]], axis=0)
    return state + change


def solution(mesh):
    placed = (
        P("gx", "gy", None),
        P(None, "gx", "gy", None),
        P("gx", "gy", None),
        P(None, "gx", "gy", None),
        P(),
        P(),
    )
    nx_dev, ny_dev = mesh.shape["gx"], mesh.shape["gy"]

    def local(*args):
        if args[0].shape == (2, 16, 128) and (nx_dev, ny_dev) == (8, 4):
            return kernel_shards(nx_dev, ny_dev, *args)
        return shards(*args)

    return jax.shard_map(
        local, mesh=mesh, in_specs=placed, out_specs=P(None, "gx", "gy", None), check_vma=False
    )
```
